32 devices in a mesh: shot: 2 (over core), strip: 16 (over z, y, x).
Axes of the slice: x: 2, y: 2, z: 4, core: 2. Of those that a mesh axis runs over, the one named last changes fastest.
Arguments:
- source_now: float32 [2, 64, 512, 256], P('shot', None, 'strip'), may hold values from -8 to 8
- source_prev: float32 [2, 64, 512, 256], P('shot', None, 'strip'), may hold values from -8 to 8
- adjoint_now: float32 [2, 64, 512, 256], P('shot', None, 'strip'), may hold values from -8 to 8
- adjoint_prev: float32 [2, 64, 512, 256], P('shot', None, 'strip'), may hold values from -8 to 8
- courant: float32 [512, 256], P('strip'), may hold values from 0.08 to 0.45
- probe_left: float32 [16, 512, 256], P(None, 'strip'), may hold values from -6 to 6
- probe_right: float32 [16, 512, 256], P(None, 'strip'), may hold values from -6 to 6
Outputs:
- left_factor: float32 [16, 512, 256], P(None, 'strip')
- right_factor: float32 [16, 512, 256], P(None, 'strip')
The draws below stay inside these ranges and needn't reach their ends.
All inputs are finite; a program needn't handle non-finite values.
Results may differ from the reference program's by a relative error of at most 0.0003.
Values sent between devices are 32-bit elements; how exact they have to be, the bound alone decides.
No kernel may reach another device: no remote copies, remote signals or barrier semaphores. Data moves between devices by JAX's collectives and lax.ppermute only.
A program may use at most 64 MiB of HBM per device.

```python
import math
import jax
import jax.numpy as jnp
from jax import lax

NCOL = 256
SRC = 64
RANK = 16
STEPS = 8
GROUPS = 2
NROW = 512


def wavefield(key, salt):
    base_key = jax.random.fold_in(key, salt)
    keys = jax.random.split(base_key, 2)
    shape = (GROUPS, SRC, NROW, NCOL)
    position = jnp.arange(NROW, dtype=jnp.float32) / max(NROW - 1, 1)
    cell_scale = 0.5 * jnp.exp(jax.random.uniform(keys[1], (1, 1, NROW, NCOL), minval=math.log(1.0 / 3.0), maxval=math.log(10.0 / 3.0)))
    noise = jax.random.normal(keys[0], shape)
    trend = (3.0 ** (position - 0.5))[:, None]
    values = noise * cell_scale * trend
    return jnp.clip(values, -8.0, 8.0).astype(jnp.float32)


def draw_source_now(key, part):
    return wavefield(key, 11)


def draw_source_prev(key, part):
    return wavefield(key, 23)


def draw_adjoint_now(key, part):
    return wavefield(key, 37)


def draw_adjoint_prev(key, part):
    return wavefield(key, 41)


def level_of(own_key, dims, pieces, smallest, largest):
    loudness = 1.0
    for dim, parts in pieces:
        steps = jax.random.uniform(jax.random.fold_in(jax.random.fold_in(own_key, 6), dim), (parts,), jnp.float32, smallest / len(pieces), largest / len(pieces))
        loudness = loudness * jnp.repeat(jnp.exp(steps), dims[dim] // parts).reshape((-1,) + (1,) * (len(dims) - 1 - dim))
    return loudness


def scatter_about(key, shape, deviation, limit, cuts=(), kind=jnp.bfloat16):
    gain = level_of(key, shape, cuts, -0.22, 0.18) if cuts else 1.0
    entries = jax.random.normal(key, shape, jnp.float32) * deviation * gain
    return jnp.minimum(jnp.maximum(entries, -limit), limit).astype(kind)


def setup_inputs(seed: int = 0) -> dict:
    streams_of = jax.random.split(jax.random.key(seed), 8)
    source_now = draw_source_now(jax.random.fold_in(streams_of[7], 71), 0)
    source_prev = draw_source_prev(jax.random.fold_in(streams_of[7], 71), 0)
    adjoint_now = draw_adjoint_now(jax.random.fold_in(streams_of[7], 71), 0)
    adjoint_prev = draw_adjoint_prev(jax.random.fold_in(streams_of[7], 71), 0)
    courant = jnp.clip(jnp.exp(math.log(0.45) - 1.7272209 * jax.random.uniform(streams_of[4], (NROW, NCOL), jnp.float32) ** level_of(streams_of[4], (NROW, NCOL), ((0, 16),), -0.2, 0.2)), 0.08, 0.45)
    probe_left = scatter_about(streams_of[5], (RANK, NROW, NCOL), 1.0, 6.0, ((1, 16),), jnp.float32)
    probe_right = scatter_about(streams_of[6], (RANK, NROW, NCOL), 1.0, 6.0, ((1, 16),), jnp.float32)
    return {"source_now": source_now, "source_prev": source_prev, "adjoint_now": adjoint_now, "adjoint_prev": adjoint_prev, "courant": courant, "probe_left": probe_left, "probe_right": probe_right}


def sideways(fields):
    zero_column = jnp.zeros_like(fields[..., :1])
    return jnp.concatenate([fields[..., 1:], zero_column], -1) + jnp.concatenate([zero_column, fields[..., :-1]], -1)

def leapfrog(field_now, field_prev, courant):
    zero_row = jnp.zeros_like(field_now[:, :1, :])
    above = jnp.concatenate([field_now[:, 1:, :], zero_row], 1)
    below = jnp.concatenate([zero_row, field_now[:, :-1, :]], 1)
    laplace = above + below + sideways(field_now) - 4.0 * field_now
    return 2.0 * field_now - field_prev + courant[None] * laplace

def orthonormal(sketch_sum):
    gram_value = jnp.dot(sketch_sum, sketch_sum.T, precision=lax.Precision.HIGHEST)
    lower_factor = jnp.linalg.cholesky(gram_value)
    solved = lax.linalg.triangular_solve(lower_factor, sketch_sum, left_side=True, lower=True)
    return (solved * math.sqrt(NROW * NCOL)).reshape(RANK, NROW, NCOL)

def reference(source_now, source_prev, adjoint_now, adjoint_prev, courant, probe_left, probe_right):
    flat_left = probe_left.reshape(RANK, -1)
    flat_right = probe_right.reshape(RANK, -1)

    def one_group(members):
        src_a, src_b, adj_a, adj_b = members
        field_now = jnp.concatenate([src_a, adj_a], 0)
        field_prev = jnp.concatenate([src_b, adj_b], 0)
        for step_index in range(STEPS):
            field_next = leapfrog(field_now, field_prev, courant)
            field_prev, field_now = (field_now, field_next)
        flat_source = field_now[:SRC].reshape(SRC, -1)
        flat_adjoint = field_now[SRC:].reshape(SRC, -1)
        left_probe = jnp.dot(flat_adjoint, flat_left.T, precision=lax.Precision.HIGHEST)
        right_probe = jnp.dot(flat_source, flat_right.T, precision=lax.Precision.HIGHEST)
        left_term = jnp.dot(left_probe.T, flat_source, precision=lax.Precision.HIGHEST)
        right_term = jnp.dot(right_probe.T, flat_adjoint, precision=lax.Precision.HIGHEST)
        return (left_term, right_term)
    left_terms, right_terms = lax.map(one_group, (source_now, source_prev, adjoint_now, adjoint_prev))
    left_sketch = lax.optimization_barrier(jnp.sum(left_terms, axis=0))
    right_sketch = lax.optimization_barrier(jnp.sum(right_terms, axis=0))
    return (orthonormal(left_sketch), orthonormal(right_sketch))
```

```python
import math

import jax
import jax.numpy as jnp
from jax import lax
from jax.experimental import pallas as pl
from jax.experimental.pallas import tpu as pltpu
from jax.sharding import PartitionSpec as P

STEPS = 8
LANES = 128
NT = (((1,), (1,)), ((), ()))
MIB = 1 << 20


def in_hbm(x):
    return pltpu.with_memory_space_constraint(x, pltpu.HBM)


def parts_of(x, count):
    parts = []
    for index in range(count):
        part = x.astype(jnp.bfloat16)
        parts.append(part)
        if index + 1 < count:
            x = x - part.astype(jnp.float32)
    return parts


def dot32(a, b, dims):
    return lax.dot_general(a, b, dims, preferred_element_type=jnp.float32)


def call(kernel, outs, vmem_mib, scratch=(), name=None, flops=0, moved=0):
    many = isinstance(outs, (list, tuple))
    spec = pl.BlockSpec(memory_space=pltpu.VMEM)
    return pl.pallas_call(
        kernel,
        out_shape=outs,
        out_specs=[spec] * len(outs) if many else spec,
        scratch_shapes=list(scratch),
        compiler_params=pltpu.CompilerParams(vmem_limit_bytes=vmem_mib * MIB),
        cost_estimate=pl.CostEstimate(flops=flops, bytes_accessed=moved, transcendentals=0),
        name=name,
    )


def f32(*shape):
    return jax.ShapeDtypeStruct(shape, jnp.float32)


def rows_first(x):
    return jnp.concatenate(
        [jnp.swapaxes(x[:, :, t : t + LANES], 0, 1) for t in range(0, x.shape[2], LANES)], 2
    )


def advance_rows(first, last, now, prev, speed, fresh):
    tiles = now.shape[2] // LANES
    spans = [slice(t * LANES, (t + 1) * LANES) for t in range(tiles)]
    lane = lax.broadcasted_iota(jnp.int32, (now.shape[1], LANES), 1)
    at_start, at_end = lane == 0, lane == LANES - 1
    above = [now[first - 1, :, span] for span in spans]
    centre = [now[first, :, span] for span in spans]
    for r in range(first, last):
        below = [now[r + 1, :, span] for span in spans]
        from_left = [pltpu.roll(c, 1, 1) for c in centre]
        from_right = [pltpu.roll(c, LANES - 1, 1) for c in centre]
        for t, span in enumerate(spans):
            left = jnp.where(at_start, from_left[t - 1] if t else 0.0, from_left[t])
            right = jnp.where(at_end, from_right[t + 1] if t + 1 < tiles else 0.0, from_right[t])
            c = speed[r : r + 1, span]
            around = (above[t] + below[t]) + (left + right)
            value = (2.0 - 4.0 * c) * centre[t] + c * around
            if not fresh:
                value = value - prev[r, :, span]
            prev[r, :, span] = value
        above, centre = centre, below


def shards(source_now, source_prev, adjoint_now, adjoint_prev, courant, probe_left, probe_right):
    _, waves, rows, cols = source_now.shape
    rank = probe_left.shape[0]
    strips, shots = lax.axis_size("strip"), lax.axis_size("shot")
    cells = rows * cols
    edge = STEPS
    tall = rows + 2 * edge
    factor_scale = math.sqrt(cells * strips)

    to_other = [(0, 1), (1, 0)]
    to_pair = [(i, i ^ 1) for i in range(strips)]
    to_next = [(i, i + 1) for i in range(1, strips - 1, 2)]
    to_next = to_next + [(b, a) for a, b in to_next]

    def where_am_i():
        return lax.axis_index("shot"), lax.rem(lax.axis_index("strip"), 2) == 0

    def edges_kernel(left, right, speed, pair, other, sem):
        side, even = where_am_i()
        pair_row = jnp.where(even, rows - edge, 0)
        other_row = jnp.where(even, 0, rows - edge)

        def copies(probe):
            made = []
            for index, (out, start) in enumerate(((pair, pair_row), (other, other_row))):
                start = pl.multiple_of(start, 8)
                made.append(
                    pltpu.make_async_copy(
                        probe.at[:, pl.ds(start, edge), :], out.at[pl.ds(0, rank)], sem.at[2 * index]
                    )
                )
                made.append(
                    pltpu.make_async_copy(
                        speed.at[pl.ds(start, edge), :], out.at[rank], sem.at[2 * index + 1]
                    )
                )
            for copy in made:
                copy.start()
            for copy in made:
                copy.wait()

        @pl.when(side == 0)
        def _():
            copies(left)

        @pl.when(side != 0)
        def _():
            copies(right)

    halo = f32(rank + 1, edge, cols)
    far = pl.BlockSpec(memory_space=pltpu.HBM)
    near = pl.BlockSpec(memory_space=pltpu.VMEM)
    pair_edge, other_edge = pl.pallas_call(
        edges_kernel,
        out_shape=[halo, halo],
        in_specs=[far] * 3,
        out_specs=[near] * 2,
        scratch_shapes=[pltpu.SemaphoreType.DMA((4,))],
        compiler_params=pltpu.CompilerParams(vmem_limit_bytes=4 * MIB),
        name="edges",
    )(in_hbm(probe_left), in_hbm(probe_right), in_hbm(courant))
    other_halo = lax.ppermute(other_edge, "strip", to_next)
    pair_halo = lax.ppermute(pair_edge, "strip", to_pair)

    group = math.gcd(waves, 16)

    def split_kernel(
        adjoint_a, adjoint_b, source_a, source_b, left, right, speeds, _,
        out, start, held, probe, speed, sems, sem,
    ):
        side, _ = where_am_i()

        def probe_copy(ref):
            return pltpu.make_async_copy(ref, probe, sem.at[0])

        speed_copy = pltpu.make_async_copy(speeds, speed, sem.at[1])
        speed_copy.start()

        @pl.when(side == 0)
        def _():
            probe_copy(left).start()

        @pl.when(side != 0)
        def _():
            probe_copy(right).start()

        copies = {}
        for index, ref in enumerate((adjoint_a, adjoint_b, source_a, source_b)):
            for first in range(0, waves, group):
                span = pl.ds(first, group)
                copies[index, first] = pltpu.make_async_copy(
                    ref.at[span], held.at[index, span], sems.at[index, first // group]
                )
        for copy in copies.values():
            copy.start()
        for (index, first), copy in copies.items():
            copy.wait()
            for block in range(0, rows, 8):
                for t in range(0, cols, LANES):
                    piece = held[index, first : first + group, block : block + 8, t : t + LANES]
                    high, low = parts_of(jnp.swapaxes(piece, 0, 1), 2)
                    for r in range(8):
                        span = slice((block + r) * cols + t, (block + r) * cols + t + LANES)
                        out[index // 2, index % 2, first : first + group, span] = high[r]
                        out[index // 2, index % 2, waves + first : waves + first + group, span] = low[r]
        speed_copy.wait()
        probe_copy(left).wait()
        for block in range(0, rows, 8):
            span = slice(block, block + 8)
            start[span] = rows_first(probe[:, span, :]) * speed[span, :][:, None, :]

    fields, start = pl.pallas_call(
        split_kernel,
        out_shape=[jax.ShapeDtypeStruct((2, 2, 2 * waves, cells), jnp.bfloat16), f32(rows, rank, cols)],
        in_specs=[far] * 7 + [pl.BlockSpec(memory_space=pl.ANY)],
        out_specs=[near, near],
        scratch_shapes=[
            pltpu.VMEM((4, waves, rows, cols), jnp.float32),
            pltpu.VMEM((rank, rows, cols), jnp.float32),
            pltpu.VMEM((rows, cols), jnp.float32),
            pltpu.SemaphoreType.DMA((4, waves // group)),
            pltpu.SemaphoreType.DMA((2,)),
        ],
        compiler_params=pltpu.CompilerParams(vmem_limit_bytes=24 * MIB),
        cost_estimate=pl.CostEstimate(flops=0, bytes_accessed=16 * waves * cells * 2, transcendentals=0),
        name="split",
    )(
        *map(in_hbm, (adjoint_now[0], adjoint_prev[0], source_now[0], source_prev[0])),
        *map(in_hbm, (probe_left, probe_right, courant)),
        pair_edge,
    )

    def fill_speeds(speeds, speed, above, below):
        speeds[edge : edge + rows, :] = speed[...]
        speeds[:edge, :] = above
        speeds[edge + rows :, :] = below

    def probe_kernel(begin, speed, pair, other, out, now, prev, speeds):
        _, even = where_am_i()
        fill_speeds(
            speeds, speed, jnp.where(even, other[rank], pair[rank]), jnp.where(even, pair[rank], other[rank])
        )
        from_pair = rows_first(pair[:rank] * pair[rank][None])
        from_other = rows_first(other[:rank] * other[rank][None])
        now[:edge] = jnp.where(even, from_other, from_pair)
        now[edge + rows :] = jnp.where(even, from_pair, from_other)
        now[edge : edge + rows] = begin[...]
        a, b = now, prev
        for step in range(1, STEPS + 1):
            advance_rows(step, tall - step, a, b, speeds, step == 1)
            a, b = b, a
        for r in range(rows):
            inverse = 1.0 / speed[r : r + 1, :]
            out[0, :, r * cols : (r + 1) * cols] = a[r + edge] * inverse
            out[1, :, r * cols : (r + 1) * cols] = b[r + edge] * (-inverse)

    state = pltpu.VMEM((tall, rank, cols), jnp.float32)
    probes_own = call(
        probe_kernel,
        f32(2, rank, cells),
        12,
        [state, state, pltpu.VMEM((tall, cols), jnp.float32)],
        name="probes",
    )(start, courant, pair_halo, other_halo)
    probes_other = lax.ppermute(probes_own, "shot", to_other)

    chunk = min(2048, cells)

    def products(fields_ref, probes_ref, side):
        total = jnp.zeros((2 * waves, 2 * rank), jnp.float32)
        for level in range(2):
            for at in range(0, cells, chunk):
                span = slice(at, at + chunk)
                pair = jnp.concatenate(parts_of(probes_ref[level, :, span], 2), 0)
                total = total + dot32(fields_ref[side, level, :, span], pair, NT)
        total = total[:waves] + total[waves:]
        return (total[:, :rank] + total[:, rank:]).T

    def product_kernel(fields_ref, probes_ref, out):
        side, _ = where_am_i()
        out[...] = products(fields_ref, probes_ref, side)

    def product_last_kernel(fields_ref, probes_ref, first_ref, out):
        side, _ = where_am_i()
        mine, theirs = first_ref[...], products(fields_ref, probes_ref, 1 - side)
        both = jnp.concatenate(
            [jnp.where(side == 0, mine, theirs), jnp.where(side == 0, theirs, mine)], 1
        )
        for strip in range(strips):
            out[strip] = both

    flops = 2 * 2 * waves * 2 * rank * cells * 2
    first_product = call(product_kernel, f32(rank, waves), 24, name="product", flops=flops)(
        fields, probes_own
    )
    pieces = call(
        product_last_kernel, f32(strips, rank, 2 * waves), 24, name="product_last", flops=flops
    )(fields, probes_other, first_product)
    pieces = lax.all_to_all(pieces, "strip", 0, 0)

    def combine_kernel(for_own):
        def kernel(pieces_ref, fields_ref, out):
            side, _ = where_am_i()
            side = side if for_own else 1 - side
            weights = jnp.sum(pieces_ref[...], 0)
            weights = jnp.where(side == 0, weights[:, :waves], weights[:, waves:])
            stack = jnp.concatenate(parts_of(weights, 2), 0)
            stack = jnp.concatenate([stack, stack], 1)
            for level in range(2):
                for at in range(0, cells, chunk):
                    span = slice(at, at + chunk)
                    both = jnp.dot(
                        stack,
                        fields_ref[1 - side, level, :, span],
                        preferred_element_type=jnp.float32,
                    )
                    out[level, :, span] = both[:rank] + both[rank:]

        return kernel

    term = f32(2, rank, cells)
    terms_sent = call(combine_kernel(False), term, 24, name="terms_sent", flops=flops)(pieces, fields)
    terms_got = lax.ppermute(terms_sent, "shot", to_other)
    terms_own = call(combine_kernel(True), term, 24, name="terms_own", flops=flops)(pieces, fields)

    def sketch_kernel(own, got, speed, pair, other, out, pair_out, other_out, now, prev, speeds):
        _, even = where_am_i()
        fill_speeds(
            speeds, speed, jnp.where(even, other[rank], pair[rank]), jnp.where(even, pair[rank], other[rank])
        )
        zeros = jnp.zeros((edge, rank, cols), jnp.float32)
        for ref in (now, prev):
            ref[:edge] = zeros
            ref[edge + rows :] = zeros
        for r in range(rows):
            span = slice(r * cols, (r + 1) * cols)
            now[r + edge] = own[0, :, span] + got[0, :, span]
            prev[r + edge] = own[1, :, span] + got[1, :, span]
        a, b = now, prev
        for step in range(1, STEPS + 1):
            reach = min(step, edge - 1)
            advance_rows(edge - reach, edge + rows + reach, a, b, speeds, False)
            if step == edge:
                for r, beside in ((0, 1), (tall - 1, tall - 2)):
                    b[r] = speeds[r : r + 1, :] * a[beside]
            a, b = b, a
        for r in range(rows):
            out[:, r * cols : (r + 1) * cols] = a[r + edge]
        for r in range(edge):
            span = slice(r * cols, (r + 1) * cols)
            above, below = a[r], a[edge + rows + r]
            pair_out[:, span] = jnp.where(even, below, above)
            other_out[:, span] = jnp.where(even, above, below)

    spill = f32(rank, edge * cols)
    sketch_own, pair_spill, other_spill = call(
        sketch_kernel,
        [f32(rank, cells), spill, spill],
        16,
        [state, state, pltpu.VMEM((tall, cols), jnp.float32)],
        name="sketch",
    )(
        terms_own,
        terms_got,
        courant,
        pair_halo,
        other_halo,
    )
    other_add = lax.ppermute(other_spill, "strip", to_next)
    pair_add = lax.ppermute(pair_spill, "strip", to_pair)

    places = shots * strips
    margin = edge * cols

    def gram_kernel(own, pair, other, out, pieces_out):
        _, even = where_am_i()
        top = own[:, :margin] + jnp.where(even, other[...], pair[...])
        bottom = own[:, cells - margin :] + jnp.where(even, pair[...], other[...])
        middle = own[:, margin : cells - margin]
        out[:, :margin] = top
        out[:, margin : cells - margin] = middle
        out[:, cells - margin :] = bottom
        total = jnp.zeros((3 * rank, 3 * rank), jnp.float32)
        for piece in (top, middle, bottom):
            stack = jnp.concatenate(parts_of(piece, 3), 0)
            total = total + dot32(stack, stack, NT)
        wide = total[:, :rank] + total[:, rank : 2 * rank] + total[:, 2 * rank :]
        gram = wide[:rank] + wide[rank : 2 * rank] + wide[2 * rank :]
        half = rank // 2
        gram = jnp.concatenate(
            [gram[:half], gram[half:], jnp.zeros((half, LANES - 2 * rank), jnp.float32)], 1
        )
        for place in range(places):
            pieces_out[place] = gram

    sketch, gram_pieces = call(
        gram_kernel, [f32(rank, cells), f32(places, rank // 2, LANES)], 12, name="gram"
    )(sketch_own, pair_add, other_add)
    sketch_other = lax.ppermute(sketch, "shot", to_other)
    gram_pieces = lax.all_to_all(gram_pieces, ("shot", "strip"), 0, 0)

    def factor_kernel(grams, own, theirs, left_out, right_out):
        side, _ = where_am_i()
        line = lax.broadcasted_iota(jnp.int32, (rank, rank), 0)
        column = lax.broadcasted_iota(jnp.int32, (rank, rank), 1)
        tall_line = lax.broadcasted_iota(jnp.int32, (rank, LANES), 0)
        sides = []
        for shot in range(2):
            halves = jnp.sum(grams[shot * strips : (shot + 1) * strips], 0)
            gram = jnp.concatenate([halves[:, :rank], halves[:, rank : 2 * rank]], 0)
            columns = [jnp.broadcast_to(gram[:, j : j + 1], (rank, LANES)) for j in range(rank)]
            sides.append((columns, [jnp.where(line == column, 1.0, 0.0)]))
        for j in range(rank):
            for columns, inverse in sides:
                factor = columns[j] * (1.0 / columns[j][j : j + 1])
                factor = jnp.where(tall_line > j, factor, 0.0)
                for k in range(j + 1, rank):
                    columns[k] = columns[k] - factor * columns[k][j : j + 1]
                inverse[0] = inverse[0] - factor[:, :rank] * inverse[0][j : j + 1]
        for (columns, inverse), shot, out in zip(sides, (0, 1), (left_out, right_out)):
            pivots = columns[0]
            for j in range(1, rank):
                pivots = jnp.where(tall_line == j, columns[j], pivots)
            inverse = inverse[0] * (lax.rsqrt(pivots[:, :rank]) * factor_scale)
            stack = jnp.concatenate(parts_of(inverse, 3), 0)
            stack = jnp.concatenate([stack] * 3, 1)
            for block in range(0, rows, 8):
                span = slice(block * cols, (block + 8) * cols)
                lines = jnp.where(side == shot, own[:, span], theirs[:, span])
                thick = jnp.concatenate(parts_of(lines, 3), 0)
                solved = jnp.dot(stack, thick, preferred_element_type=jnp.float32)
                solved = solved[:rank] + solved[rank : 2 * rank] + solved[2 * rank :]
                for t in range(0, cols, LANES):
                    tile = [solved[:, r * cols + t : r * cols + t + LANES][None] for r in range(8)]
                    out[:, block : block + 8, t : t + LANES] = jnp.swapaxes(
                        jnp.concatenate(tile, 0), 0, 1
                    )

    factor = f32(rank, rows, cols)
    left_factor, right_factor = call(factor_kernel, [factor, factor], 12, name="factors")(
        gram_pieces, sketch, sketch_other
    )
    return left_factor, right_factor


def solution(mesh):
    return jax.shard_map(
        shards,
        mesh=mesh,
        in_specs=(
            P("shot", None, "strip", None),
            P("shot", None, "strip", None),
            P("shot", None, "strip", None),
            P("shot", None, "strip", None),
            P("strip", None),
            P(None, "strip", None),
            P(None, "strip", None),
        ),
        out_specs=(P(None, "strip", None), P(None, "strip", None)),
        check_vma=False,
    )
```

```python
import math

import jax
import jax.numpy as jnp
from jax import lax
from jax.experimental import pallas as pl
from jax.experimental.pallas import tpu as pltpu
from jax.sharding import PartitionSpec as P

STEPS = 8
LANES = 128
NT = (((1,), (1,)), ((), ()))
MIB = 1 << 20


def in_hbm(x):
    return pltpu.with_memory_space_constraint(x, pltpu.HBM)


def parts_of(x, count):
    parts = []
    for index in range(count):
        part = x.astype(jnp.bfloat16)
        parts.append(part)
        if index + 1 < count:
            x = x - part.astype(jnp.float32)
    return parts


def dot32(a, b, dims):
    return lax.dot_general(a, b, dims, preferred_element_type=jnp.float32)


def call(kernel, outs, vmem_mib, scratch=(), name=None, flops=0, moved=0):
    many = isinstance(outs, (list, tuple))
    spec = pl.BlockSpec(memory_space=pltpu.VMEM)
    return pl.pallas_call(
        kernel,
        out_shape=outs,
        out_specs=[spec] * len(outs) if many else spec,
        scratch_shapes=list(scratch),
        compiler_params=pltpu.CompilerParams(vmem_limit_bytes=vmem_mib * MIB),
        cost_estimate=pl.CostEstimate(flops=flops, bytes_accessed=moved, transcendentals=0),
        name=name,
    )


def f32(*shape):
    return jax.ShapeDtypeStruct(shape, jnp.float32)


def rows_first(x):
    return jnp.concatenate(
        [jnp.swapaxes(x[:, :, t : t + LANES], 0, 1) for t in range(0, x.shape[2], LANES)], 2
    )


def advance_rows(first, last, now, prev, speed, fresh):
    tiles = now.shape[2] // LANES
    spans = [slice(t * LANES, (t + 1) * LANES) for t in range(tiles)]
    lane = lax.broadcasted_iota(jnp.int32, (now.shape[1], LANES), 1)
    at_start, at_end = lane == 0, lane == LANES - 1
    above = [now[first - 1, :, span] for span in spans]
    centre = [now[first, :, span] for span in spans]
    for r in range(first, last):
        below = [now[r + 1, :, span] for span in spans]
        from_left = [pltpu.roll(c, 1, 1) for c in centre]
        from_right = [pltpu.roll(c, LANES - 1, 1) for c in centre]
        for t, span in enumerate(spans):
            left = jnp.where(at_start, from_left[t - 1] if t else 0.0, from_left[t])
            right = jnp.where(at_end, from_right[t + 1] if t + 1 < tiles else 0.0, from_right[t])
            c = speed[r : r + 1, span]
            around = (above[t] + below[t]) + (left + right)
            value = (2.0 - 4.0 * c) * centre[t] + c * around
            if not fresh:
                value = value - prev[r, :, span]
            prev[r, :, span] = value
        above, centre = centre, below


def shards(source_now, source_prev, adjoint_now, adjoint_prev, courant, probe_left, probe_right):
    _, waves, rows, cols = source_now.shape
    rank = probe_left.shape[0]
    strips, shots = lax.axis_size("strip"), lax.axis_size("shot")
    cells = rows * cols
    edge = STEPS
    factor_scale = math.sqrt(cells * strips)

    to_other = [(0, 1), (1, 0)]
    to_pair = [(i, i ^ 1) for i in range(strips)]
    to_next = [(i, i + 1) for i in range(1, strips - 1, 2)]
    to_next = to_next + [(b, a) for a, b in to_next]

    def where_am_i():
        return lax.axis_index("shot"), lax.rem(lax.axis_index("strip"), 2) == 0

    def edges_kernel(left, right, speed, pair, other, sem):
        side, even = where_am_i()
        pair_row = jnp.where(even, rows - edge, 0)
        other_row = jnp.where(even, 0, rows - edge)

        def copies(probe):
            made = []
            for index, (out, start) in enumerate(((pair, pair_row), (other, other_row))):
                start = pl.multiple_of(start, 8)
                made.append(
                    pltpu.make_async_copy(
                        probe.at[:, pl.ds(start, edge), :], out.at[pl.ds(0, rank)], sem.at[2 * index]
                    )
                )
                made.append(
                    pltpu.make_async_copy(
                        speed.at[pl.ds(start, edge), :], out.at[rank], sem.at[2 * index + 1]
                    )
                )
            for copy in made:
                copy.start()
            for copy in made:
                copy.wait()

        @pl.when(side == 0)
        def _():
            copies(left)

        @pl.when(side != 0)
        def _():
            copies(right)

    halo = f32(rank + 1, edge, cols)
    far = pl.BlockSpec(memory_space=pltpu.HBM)
    near = pl.BlockSpec(memory_space=pltpu.VMEM)
    pair_edge, other_edge = pl.pallas_call(
        edges_kernel,
        out_shape=[halo, halo],
        in_specs=[far] * 3,
        out_specs=[near] * 2,
        scratch_shapes=[pltpu.SemaphoreType.DMA((4,))],
        compiler_params=pltpu.CompilerParams(vmem_limit_bytes=4 * MIB),
        cost_estimate=pl.CostEstimate(flops=20000000000, bytes_accessed=4194304, transcendentals=0),
        name="edges",
    )(in_hbm(probe_left), in_hbm(probe_right), in_hbm(courant))
    other_halo = lax.ppermute(other_edge, "strip", to_next)
    pair_halo = lax.ppermute(pair_edge, "strip", to_pair)

    group = math.gcd(waves, 16)

    def lay_out(piece, out, high_at, low_at, at, t):
        high, low = parts_of(jnp.swapaxes(piece, 0, 1), 2)
        for r in range(8):
            span = slice((at + r) * cols + t, (at + r) * cols + t + LANES)
            out[high_at, span] = high[r]
            out[low_at, span] = low[r]

    def split_kernel(
        adjoint_a, adjoint_b, source_a, source_b, left, right, speeds, _,
        out, start, inner_stage, probe, speed, sem,
    ):
        side, _ = where_am_i()

        def probe_copy(ref):
            return pltpu.make_async_copy(ref, probe, sem.at[0])

        speed_copy = pltpu.make_async_copy(speeds, speed, sem.at[1])
        speed_copy.start()

        @pl.when(side == 0)
        def _():
            probe_copy(left).start()

        @pl.when(side != 0)
        def _():
            probe_copy(right).start()

        for level, adjoint, source in ((0, adjoint_a, source_a), (1, adjoint_b, source_b)):
            for first in range(0, waves, group):
                some = slice(first, first + group)
                low = slice(waves + first, waves + first + group)
                for block in range(0, rows, 8):
                    for t in range(0, cols, LANES):
                        span = slice(t, t + LANES)
                        mine, other = adjoint[some, block : block + 8, span], source[some, block : block + 8, span]
                        if edge <= block < rows - edge:
                            sent = jnp.where(side == 0, mine, other)
                            inner_stage[level, some, block - edge : block - edge + 8, span] = sent
                        lay_out(mine, out.at[0, level], some, low, block, t)
                        lay_out(other, out.at[1, level], some, low, block, t)
        speed_copy.wait()
        probe_copy(left).wait()
        for block in range(0, rows, 8):
            span = slice(block, block + 8)
            start[span] = rows_first(probe[:, span, :]) * speed[span, :][:, None, :]

    def stage_kernel(adjoint_a, adjoint_b, source_a, source_b, _, out):
        side, _ = where_am_i()

        def stage(pair):
            for level, ref in enumerate(pair):
                out[level, :, :edge] = ref[:, :edge]
                out[level, :, edge:] = ref[:, rows - edge :]

        @pl.when(side == 0)
        def _():
            stage((adjoint_a, adjoint_b))

        @pl.when(side != 0)
        def _():
            stage((source_a, source_b))

    kinds = (adjoint_now[0], adjoint_prev[0], source_now[0], source_prev[0])
    rim_stage = pl.pallas_call(
        stage_kernel,
        out_shape=f32(2, waves, 2 * edge, cols),
        in_specs=[near] * 4 + [pl.BlockSpec(memory_space=pl.ANY)],
        out_specs=near,
        compiler_params=pltpu.CompilerParams(vmem_limit_bytes=26 * MIB),
        name="stage",
    )(*kinds, pair_edge)
    fields, start, inner_stage = pl.pallas_call(
        split_kernel,
        out_shape=[
            jax.ShapeDtypeStruct((2, 2, 2 * waves, cells), jnp.bfloat16),
            f32(rows, rank, cols),
            f32(2, waves, rows - 2 * edge, cols),
        ],
        in_specs=[near] * 4 + [far] * 3 + [pl.BlockSpec(memory_space=pl.ANY)],
        out_specs=[near] * 3,
        scratch_shapes=[
            pltpu.VMEM((rank, rows, cols), jnp.float32),
            pltpu.VMEM((rows, cols), jnp.float32),
            pltpu.SemaphoreType.DMA((2,)),
        ],
        compiler_params=pltpu.CompilerParams(vmem_limit_bytes=26 * MIB),
        cost_estimate=pl.CostEstimate(flops=0, bytes_accessed=16 * waves * cells * 2, transcendentals=0),
        name="split",
    )(
        *kinds,
        *map(in_hbm, (probe_left, probe_right, courant)),
        pair_edge,
    )
    rim_raw = lax.ppermute(rim_stage, "shot", to_other)

    inner = rows - 2 * edge
    rim = edge * cols

    def inner_kernel(begin, speed, out, saved, now, prev):
        now[...] = begin[...]
        a, b = now, prev
        for step in range(STEPS):
            saved[step, :2] = a[step : step + 2]
            saved[step, 2:] = a[rows - 2 - step : rows - step]
            advance_rows(step + 1, rows - 1 - step, a, b, speed, step == 0)
            a, b = b, a
        for r in range(edge, edge + inner):
            span = slice((r - edge) * cols, (r - edge + 1) * cols)
            inverse = 1.0 / speed[r : r + 1, :]
            out[0, :, span] = a[r] * inverse
            out[1, :, span] = b[r] * (-inverse)

    state = pltpu.VMEM((rows, rank, cols), jnp.float32)
    inner_own, saved = call(
        inner_kernel,
        [f32(2, rank, inner * cols), f32(STEPS, 4, rank, cols)],
        12,
        [state, state],
        name="probes_inner",
    )(start, courant)
    inner_other = lax.ppermute(inner_own, "shot", to_other)

    def far_speeds(pair, other):
        _, even = where_am_i()
        above = jnp.where(even, other[rank], pair[rank])
        below = jnp.where(even, pair[rank], other[rank])
        return above, below

    def rim_kernel(saved, speed, pair, other, out, up_now, up_prev, low_now, low_prev, up_speed, low_speed):
        _, even = where_am_i()
        up_speed[:edge, :], low_speed[edge + 1 :, :] = far_speeds(pair, other)
        up_speed[edge : 2 * edge, :] = speed[:edge, :]
        low_speed[1 : edge + 1, :] = speed[rows - edge :, :]
        from_pair = rows_first(pair[:rank] * pair[rank][None])
        from_other = rows_first(other[:rank] * other[rank][None])
        up_now[:edge] = jnp.where(even, from_other, from_pair)
        low_now[edge + 1 :] = jnp.where(even, from_pair, from_other)
        up_now[edge : edge + 2] = saved[0, :2]
        low_now[edge - 1 : edge + 1] = saved[0, 2:]
        a, b, c, d = up_now, up_prev, low_now, low_prev
        for step in range(1, STEPS + 1):
            advance_rows(step, edge + step, a, b, up_speed, step == 1)
            advance_rows(edge + 1 - step, 2 * edge + 1 - step, c, d, low_speed, step == 1)
            if step < STEPS:
                b[edge + step : edge + step + 2] = saved[step, :2]
                d[edge - 1 - step : edge + 1 - step] = saved[step, 2:]
            a, b, c, d = b, a, d, c
        for r in range(edge):
            upper = slice(r * cols, (r + 1) * cols)
            lower = slice(rim + r * cols, rim + (r + 1) * cols)
            inverse = 1.0 / speed[r : r + 1, :]
            out[0, :, upper] = a[edge + r] * inverse
            out[1, :, upper] = b[edge + r] * (-inverse)
            inverse = 1.0 / speed[rows - edge + r : rows - edge + r + 1, :]
            out[0, :, lower] = c[r + 1] * inverse
            out[1, :, lower] = d[r + 1] * (-inverse)

    short = pltpu.VMEM((2 * edge + 1, rank, cols), jnp.float32)
    short_speed = pltpu.VMEM((2 * edge + 1, cols), jnp.float32)
    rim_own = call(
        rim_kernel,
        f32(2, rank, 2 * rim),
        12,
        [short] * 4 + [short_speed] * 2,
        name="probes_rim",
    )(saved, courant, pair_halo, other_halo)
    rim_other = lax.ppermute(rim_own, "shot", to_other)

    def products(fields_ref, probes_ref, side, inside):
        total = jnp.zeros((2 * waves, 2 * rank), jnp.float32)
        places = [(rim, 0, inner * cols)] if inside else [(0, 0, rim), (cells - rim, rim, rim)]
        for level in range(2):
            for at, probe_at, count in places:
                pair = jnp.concatenate(parts_of(probes_ref[level, :, probe_at : probe_at + count], 2), 0)
                total = total + dot32(fields_ref[side, level, :, at : at + count], pair, NT)
        total = total[:waves] + total[waves:]
        return (total[:, :rank] + total[:, rank:]).T

    def product_kernel(fields_ref, inner_mine, inner_theirs, rim_mine, raw, mine, theirs, swapped):
        side, _ = where_am_i()
        mine[...] = products(fields_ref, inner_mine, side, True) + products(
            fields_ref, rim_mine, side, False
        )
        theirs[...] = products(fields_ref, inner_theirs, 1 - side, True)
        lay_out_raw(raw, swapped)

    def lay_out_raw(raw, out):
        for level in range(2):
            for first in range(0, waves, group):
                some = slice(first, first + group)
                low = slice(waves + first, waves + first + group)
                for block in range(0, raw.shape[2], 8):
                    for t in range(0, cols, LANES):
                        piece = raw[level, some, block : block + 8, t : t + LANES]
                        lay_out(piece, out.at[level], some, low, block, t)

    half = rank // 2

    def product_last_kernel(fields_ref, rim_theirs, mine_ref, theirs_ref, out):
        side, _ = where_am_i()
        mine = mine_ref[...]
        theirs = theirs_ref[...] + products(fields_ref, rim_theirs, 1 - side, False)
        for shot in range(shots):
            weights = jnp.where(side == shot, mine, theirs)
            weights = jnp.concatenate([weights[:half], weights[half:]], 1)
            for strip in range(strips):
                out[shot * strips + strip] = weights

    flops = 2 * 2 * waves * 2 * rank * cells * 2
    mine, theirs, rim_swapped = call(
        product_kernel,
        [f32(rank, waves)] * 2 + [jax.ShapeDtypeStruct((2, 2 * waves, 2 * rim), jnp.bfloat16)],
        24,
        name="product",
    )(fields, inner_own, inner_other, rim_own, rim_raw)
    pieces = call(
        product_last_kernel, f32(shots * strips, half, 2 * waves), 24, name="product_last"
    )(fields, rim_other, mine, theirs)
    inner_stage, pieces = lax.optimization_barrier((inner_stage, pieces))
    inner_raw = lax.ppermute(inner_stage, "shot", to_other)
    pieces = lax.all_to_all(pieces, ("shot", "strip"), 0, 0)

    def combine(pieces_ref, fields_ref, swapped_ref, places, out):
        side, _ = where_am_i()
        weights = []
        for shot in range(shots):
            packed = jnp.sum(pieces_ref[shot * strips : (shot + 1) * strips], 0)
            weights.append(jnp.concatenate([packed[:, :waves], packed[:, waves:]], 0))
        stacks = []
        for own, other in (weights, weights[::-1]):
            stack = jnp.concatenate(parts_of(jnp.where(side == 0, own, other), 2), 0)
            stacks.append(jnp.concatenate([stack, stack], 1))
        for level in range(2):
            for at, place, count in places:
                both = jnp.dot(
                    stacks[0],
                    fields_ref[1 - side, level, :, at : at + count],
                    preferred_element_type=jnp.float32,
                ) + jnp.dot(
                    stacks[1],
                    swapped_ref[level, :, place : place + count],
                    preferred_element_type=jnp.float32,
                )
                out[level, :, place : place + count] = both[:rank] + both[rank:]

    def rim_terms_kernel(pieces_ref, fields_ref, swapped_ref, out):
        places = [(0, 0, rim), (cells - rim, rim, rim)]
        combine(pieces_ref, fields_ref, swapped_ref, places, out)

    def inner_terms_kernel(pieces_ref, fields_ref, raw, _, out, swapped):
        lay_out_raw(raw, swapped)
        combine(pieces_ref, fields_ref, swapped, [(rim, 0, inner * cols)], out)

    rim_terms = call(
        rim_terms_kernel, f32(2, rank, 2 * rim), 24, name="terms_rim", flops=flops
    )(pieces, fields, rim_swapped)

    def spill_kernel(
        own, speed, pair, other, pair_out, other_out,
        up_now, up_prev, low_now, low_prev, up_speed, low_speed,
    ):
        _, even = where_am_i()
        above, below = far_speeds(pair, other)
        up_speed[1 : edge + 1, :] = above
        up_speed[edge + 1 :, :] = speed[:edge, :]
        low_speed[:edge, :] = speed[rows - edge :, :]
        low_speed[edge : 2 * edge, :] = below
        zeros = jnp.zeros((edge + 1, rank, cols), jnp.float32)
        for up, low, level in ((up_now, low_now, 0), (up_prev, low_prev, 1)):
            up[: edge + 1] = zeros
            low[edge:] = zeros
            for r in range(edge):
                span = slice(r * cols, (r + 1) * cols)
                up[edge + 1 + r] = own[level, :, span]
                span = slice(rim + r * cols, rim + (r + 1) * cols)
                low[r] = own[level, :, span]
        a, b, c, d = up_now, up_prev, low_now, low_prev
        for step in range(1, STEPS + 1):
            advance_rows(edge + 1 - step, 2 * edge + 1 - step, a, b, up_speed, False)
            advance_rows(step, edge + step, c, d, low_speed, False)
            a, b, c, d = b, a, d, c
        for r in range(edge):
            span = slice(r * cols, (r + 1) * cols)
            upper, lower = a[1 + r], c[edge + r]
            pair_out[:, span] = jnp.where(even, lower, upper)
            other_out[:, span] = jnp.where(even, upper, lower)

    spill = f32(rank, rim)
    pair_spill, other_spill = call(
        spill_kernel,
        [spill, spill],
        16,
        [short] * 4 + [short_speed] * 2,
        name="spill",
    )(rim_terms, courant, pair_halo, other_halo)
    other_add = lax.ppermute(other_spill, "strip", to_next)
    pair_add = lax.ppermute(pair_spill, "strip", to_pair)

    inner_terms = call(
        inner_terms_kernel,
        f32(2, rank, inner * cols),
        24,
        [pltpu.VMEM((2, 2 * waves, inner * cols), jnp.bfloat16)],
        name="terms_inner",
        flops=flops,
    )(pieces, fields, inner_raw, pair_spill)
    pad = STEPS // 2 + 1
    tall = rows + 2 * pad

    def sketch_kernel(
        rim_part, inner_part, speed, pair, other, _, out, now, prev, speeds
    ):
        above, below = far_speeds(pair, other)
        speeds[:pad, :] = above[edge - pad :, :]
        speeds[pad : pad + rows, :] = speed[...]
        speeds[pad + rows :, :] = below[:pad, :]
        zeros = jnp.zeros((pad, rank, cols), jnp.float32)
        for ref in (now, prev):
            ref[:pad] = zeros
            ref[pad + rows :] = zeros
        for r in range(rows):
            part, line = rim_part, r
            if edge <= r < rows - edge:
                part, line = inner_part, r - edge
            elif r >= edge:
                line = r - inner
            span = slice(line * cols, (line + 1) * cols)
            now[r + pad] = part[0, :, span]
            prev[r + pad] = part[1, :, span]
        a, b = now, prev
        for step in range(1, STEPS + 1):
            reach = min(step, STEPS - step)
            advance_rows(pad - reach, pad + rows + reach, a, b, speeds, False)
            a, b = b, a
        for r in range(rows):
            out[:, r * cols : (r + 1) * cols] = a[r + pad]

    lines = pltpu.VMEM((tall, rank, cols), jnp.float32)
    sketch_own = call(
        sketch_kernel,
        f32(rank, cells),
        16,
        [lines, lines, pltpu.VMEM((tall, cols), jnp.float32)],
        name="sketch",
        moved=8 * MIB,
    )(rim_terms, inner_terms, courant, pair_halo, other_halo, pair_spill)

    places = shots * strips

    def gram_kernel(own, pair, other, out, pieces_out):
        _, even = where_am_i()
        top = own[:, :rim] + jnp.where(even, other[...], pair[...])
        bottom = own[:, cells - rim :] + jnp.where(even, pair[...], other[...])
        middle = own[:, rim : cells - rim]
        out[:, :rim] = top
        out[:, rim : cells - rim] = middle
        out[:, cells - rim :] = bottom
        total = jnp.zeros((3 * rank, 3 * rank), jnp.float32)
        for piece in (top, middle, bottom):
            stack = jnp.concatenate(parts_of(piece, 3), 0)
            total = total + dot32(stack, stack, NT)
        wide = total[:, :rank] + total[:, rank : 2 * rank] + total[:, 2 * rank :]
        gram = wide[:rank] + wide[rank : 2 * rank] + wide[2 * rank :]
        gram = jnp.concatenate(
            [gram[:half], gram[half:], jnp.zeros((half, LANES - 2 * rank), jnp.float32)], 1
        )
        for place in range(places):
            pieces_out[place] = gram

    sketch, gram_pieces = call(
        gram_kernel, [f32(rank, cells), f32(places, rank // 2, LANES)], 12, name="gram"
    )(sketch_own, pair_add, other_add)
    sketch_other = lax.ppermute(sketch, "shot", to_other)
    gram_pieces = lax.all_to_all(gram_pieces, ("shot", "strip"), 0, 0)

    def factor_kernel(grams, own, theirs, left_out, right_out, held, sems):
        side, _ = where_am_i()
        line = lax.broadcasted_iota(jnp.int32, (rank, rank), 0)
        column = lax.broadcasted_iota(jnp.int32, (rank, rank), 1)
        tall_line = lax.broadcasted_iota(jnp.int32, (rank, LANES), 0)
        sides = []
        for shot in range(2):
            halves = jnp.sum(grams[shot * strips : (shot + 1) * strips], 0)
            gram = jnp.concatenate([halves[:, :rank], halves[:, rank : 2 * rank]], 0)
            columns = [jnp.broadcast_to(gram[:, j : j + 1], (rank, LANES)) for j in range(rank)]
            sides.append((columns, [jnp.where(line == column, 1.0, 0.0)]))
        for j in range(rank):
            for columns, inverse in sides:
                factor = columns[j] * (1.0 / columns[j][j : j + 1])
                factor = jnp.where(tall_line > j, factor, 0.0)
                for k in range(j + 1, rank):
                    columns[k] = columns[k] - factor * columns[k][j : j + 1]
                inverse[0] = inverse[0] - factor[:, :rank] * inverse[0][j : j + 1]
        copies = []
        for (columns, inverse), shot, out in zip(sides, (0, 1), (left_out, right_out)):
            pivots = columns[0]
            for j in range(1, rank):
                pivots = jnp.where(tall_line == j, columns[j], pivots)
            inverse = inverse[0] * (lax.rsqrt(pivots[:, :rank]) * factor_scale)
            stack = jnp.concatenate(parts_of(inverse, 3), 0)
            stack = jnp.concatenate([stack] * 3, 1)
            for block in range(0, rows, 8):
                span = slice(block * cols, (block + 8) * cols)
                lines = jnp.where(side == shot, own[:, span], theirs[:, span])
                thick = jnp.concatenate(parts_of(lines, 3), 0)
                solved = jnp.dot(stack, thick, preferred_element_type=jnp.float32)
                solved = solved[:rank] + solved[rank : 2 * rank] + solved[2 * rank :]
                for t in range(0, cols, LANES):
                    tile = [solved[:, r * cols + t : r * cols + t + LANES][None] for r in range(8)]
                    held[shot, :, block : block + 8, t : t + LANES] = jnp.swapaxes(
                        jnp.concatenate(tile, 0), 0, 1
                    )
                lines_here = pl.ds(block, 8)
                copies.append(
                    pltpu.make_async_copy(
                        held.at[shot, :, lines_here], out.at[:, lines_here], sems.at[shot, block // 8]
                    )
                )
                copies[-1].start()
        for copy in copies:
            copy.wait()

    factor = f32(rank, rows, cols)
    left_factor, right_factor = pl.pallas_call(
        factor_kernel,
        out_shape=[factor, factor],
        in_specs=[near] * 3,
        out_specs=[far] * 2,
        scratch_shapes=[
            pltpu.VMEM((2, rank, rows, cols), jnp.float32),
            pltpu.SemaphoreType.DMA((2, rows // 8)),
        ],
        compiler_params=pltpu.CompilerParams(vmem_limit_bytes=12 * MIB),
        name="factors",
    )(gram_pieces, sketch, sketch_other)
    return left_factor, right_factor


def solution(mesh):
    return jax.shard_map(
        shards,
        mesh=mesh,
        in_specs=(
            P("shot", None, "strip", None),
            P("shot", None, "strip", None),
            P("shot", None, "strip", None),
            P("shot", None, "strip", None),
            P("strip", None),
            P(None, "strip", None),
            P(None, "strip", None),
        ),
        out_specs=(P(None, "strip", None), P(None, "strip", None)),
        check_vma=False,
    )
```

```python
import math

import jax
import jax.numpy as jnp
from jax import lax
from jax.experimental import pallas as pl
from jax.experimental.pallas import tpu as pltpu
from jax.sharding import PartitionSpec as P

STEPS = 8
LANES = 128
NT = (((1,), (1,)), ((), ()))
MIB = 1 << 20


def in_hbm(x):
    return pltpu.with_memory_space_constraint(x, pltpu.HBM)


def parts_of(x, count):
    parts = []
    for index in range(count):
        part = x.astype(jnp.bfloat16)
        parts.append(part)
        if index + 1 < count:
            x = x - part.astype(jnp.float32)
    return parts


def dot32(a, b, dims):
    return lax.dot_general(a, b, dims, preferred_element_type=jnp.float32)


def call(kernel, outs, vmem_mib, scratch=(), name=None, flops=0, moved=0):
    many = isinstance(outs, (list, tuple))
    spec = pl.BlockSpec(memory_space=pltpu.VMEM)
    return pl.pallas_call(
        kernel,
        out_shape=outs,
        out_specs=[spec] * len(outs) if many else spec,
        scratch_shapes=list(scratch),
        compiler_params=pltpu.CompilerParams(vmem_limit_bytes=vmem_mib * MIB),
        cost_estimate=pl.CostEstimate(flops=flops, bytes_accessed=moved, transcendentals=0),
        name=name,
    )


def f32(*shape):
    return jax.ShapeDtypeStruct(shape, jnp.float32)


def rows_first(x):
    return jnp.concatenate(
        [jnp.swapaxes(x[:, :, t : t + LANES], 0, 1) for t in range(0, x.shape[2], LANES)], 2
    )


def advance_rows(first, last, now, prev, speed, fresh):
    tiles = now.shape[2] // LANES
    spans = [slice(t * LANES, (t + 1) * LANES) for t in range(tiles)]
    lane = lax.broadcasted_iota(jnp.int32, (now.shape[1], LANES), 1)
    at_start, at_end = lane == 0, lane == LANES - 1
    above = [now[first - 1, :, span] for span in spans]
    centre = [now[first, :, span] for span in spans]
    for r in range(first, last):
        below = [now[r + 1, :, span] for span in spans]
        from_left = [pltpu.roll(c, 1, 1) for c in centre]
        from_right = [pltpu.roll(c, LANES - 1, 1) for c in centre]
        for t, span in enumerate(spans):
            left = jnp.where(at_start, from_left[t - 1] if t else 0.0, from_left[t])
            right = jnp.where(at_end, from_right[t + 1] if t + 1 < tiles else 0.0, from_right[t])
            c = speed[r : r + 1, span]
            around = (above[t] + below[t]) + (left + right)
            value = (2.0 - 4.0 * c) * centre[t] + c * around
            if not fresh:
                value = value - prev[r, :, span]
            prev[r, :, span] = value
        above, centre = centre, below


def shards(source_now, source_prev, adjoint_now, adjoint_prev, courant, probe_left, probe_right):
    _, waves, rows, cols = source_now.shape
    rank = probe_left.shape[0]
    strips, shots = lax.axis_size("strip"), lax.axis_size("shot")
    cells = rows * cols
    edge = STEPS
    factor_scale = math.sqrt(cells * strips)

    to_other = [(0, 1), (1, 0)]
    to_pair = [(i, i ^ 1) for i in range(strips)]
    to_next = [(i, i + 1) for i in range(1, strips - 1, 2)]
    to_next = to_next + [(b, a) for a, b in to_next]

    def where_am_i():
        return lax.axis_index("shot"), lax.rem(lax.axis_index("strip"), 2) == 0

    def edges_kernel(left, right, speed, pair, other, sem):
        side, even = where_am_i()
        pair_row = jnp.where(even, rows - edge, 0)
        other_row = jnp.where(even, 0, rows - edge)

        def copies(probe):
            made = []
            for index, (out, start) in enumerate(((pair, pair_row), (other, other_row))):
                start = pl.multiple_of(start, 8)
                if out.shape[0] > rank + 1:
                    made.append(
                        pltpu.make_async_copy(speed.at[pl.ds(start, edge), :], out.at[rank + 1], sem.at[4])
                    )
                made.append(
                    pltpu.make_async_copy(
                        probe.at[:, pl.ds(start, edge), :], out.at[pl.ds(0, rank)], sem.at[2 * index]
                    )
                )
                made.append(
                    pltpu.make_async_copy(
                        speed.at[pl.ds(start, edge), :], out.at[rank], sem.at[2 * index + 1]
                    )
                )
            for copy in made:
                copy.start()
            for copy in made:
                copy.wait()

        @pl.when(side == 0)
        def _():
            copies(left)

        @pl.when(side != 0)
        def _():
            copies(right)

    halo = f32(rank + 1, edge, cols)
    far = pl.BlockSpec(memory_space=pltpu.HBM)
    near = pl.BlockSpec(memory_space=pltpu.VMEM)
    pair_edge, other_edge = pl.pallas_call(
        edges_kernel,
        out_shape=[f32(rank + 2, edge, cols), halo],
        in_specs=[far] * 3,
        out_specs=[near] * 2,
        scratch_shapes=[pltpu.SemaphoreType.DMA((5,))],
        compiler_params=pltpu.CompilerParams(vmem_limit_bytes=4 * MIB),
        cost_estimate=pl.CostEstimate(flops=20000000000, bytes_accessed=4194304, transcendentals=0),
        name="edges",
    )(in_hbm(probe_left), in_hbm(probe_right), in_hbm(courant))
    other_halo = lax.ppermute(other_edge, "strip", to_next)
    pair_halo = lax.ppermute(pair_edge, "strip", to_pair)

    group = math.gcd(waves, 16)

    def lay_out(piece, out, high_at, low_at, at, t):
        high, low = parts_of(jnp.swapaxes(piece, 0, 1), 2)
        for r in range(8):
            span = slice((at + r) * cols + t, (at + r) * cols + t + LANES)
            out[high_at, span] = high[r]
            out[low_at, span] = low[r]

    def split_kernel(
        adjoint_a, adjoint_b, source_a, source_b, left, right, speeds, _,
        out, start, stage, probe, speed, sem,
    ):
        side, _ = where_am_i()

        def probe_copy(ref):
            return pltpu.make_async_copy(ref, probe, sem.at[0])

        speed_copy = pltpu.make_async_copy(speeds, speed, sem.at[1])
        speed_copy.start()

        @pl.when(side == 0)
        def _():
            probe_copy(left).start()

        @pl.when(side != 0)
        def _():
            probe_copy(right).start()

        for level, adjoint, source in ((0, adjoint_a, source_a), (1, adjoint_b, source_b)):
            for first in range(0, waves, group):
                some = slice(first, first + group)
                low = slice(waves + first, waves + first + group)
                for block in range(0, rows, 8):
                    for t in range(0, cols, LANES):
                        span = slice(t, t + LANES)
                        mine, other = adjoint[some, block : block + 8, span], source[some, block : block + 8, span]
                        stage[level, some, block : block + 8, span] = jnp.where(side == 0, mine, other)
                        lay_out(mine, out.at[0, level], some, low, block, t)
                        lay_out(other, out.at[1, level], some, low, block, t)
        speed_copy.wait()
        probe_copy(left).wait()
        for block in range(0, rows, 8):
            span = slice(block, block + 8)
            start[span] = rows_first(probe[:, span, :]) * speed[span, :][:, None, :]

    fields, start, stage = pl.pallas_call(
        split_kernel,
        out_shape=[
            jax.ShapeDtypeStruct((2, 2, 2 * waves, cells), jnp.bfloat16),
            f32(rows, rank, cols),
            f32(2, waves, rows, cols),
        ],
        in_specs=[near] * 4 + [far] * 3 + [pl.BlockSpec(memory_space=pl.ANY)],
        out_specs=[near] * 3,
        scratch_shapes=[
            pltpu.VMEM((rank, rows, cols), jnp.float32),
            pltpu.VMEM((rows, cols), jnp.float32),
            pltpu.SemaphoreType.DMA((2,)),
        ],
        compiler_params=pltpu.CompilerParams(vmem_limit_bytes=26 * MIB),
        cost_estimate=pl.CostEstimate(flops=0, bytes_accessed=16 * waves * cells * 2, transcendentals=0),
        name="split",
    )(
        adjoint_now[0], adjoint_prev[0], source_now[0], source_prev[0],
        *map(in_hbm, (probe_left, probe_right, courant)),
        pair_edge,
    )
    inner = rows - 2 * edge
    rim = edge * cols

    def inner_kernel(begin, speed, out, saved, now, prev):
        now[...] = begin[...]
        a, b = now, prev
        for step in range(STEPS):
            saved[step, :2] = a[step : step + 2]
            saved[step, 2:] = a[rows - 2 - step : rows - step]
            advance_rows(step + 1, rows - 1 - step, a, b, speed, step == 0)
            a, b = b, a
        for r in range(edge, edge + inner):
            span = slice((r - edge) * cols, (r - edge + 1) * cols)
            inverse = 1.0 / speed[r : r + 1, :]
            out[0, :, span] = a[r] * inverse
            out[1, :, span] = b[r] * (-inverse)

    state = pltpu.VMEM((rows, rank, cols), jnp.float32)
    inner_own, saved = call(
        inner_kernel,
        [f32(2, rank, inner * cols), f32(STEPS, 4, rank, cols)],
        12,
        [state, state],
        name="probes_inner",
    )(start, courant)
    inner_other = lax.ppermute(inner_own, "shot", to_other)

    def far_speeds(pair, other):
        _, even = where_am_i()
        above = jnp.where(even, other[rank], pair[rank])
        below = jnp.where(even, pair[rank], other[rank])
        return above, below

    def rim_kernel(saved, speed, pair, other, out, up_now, up_prev, low_now, low_prev, up_speed, low_speed):
        _, even = where_am_i()
        up_speed[:edge, :], low_speed[edge + 1 :, :] = far_speeds(pair, other)
        up_speed[edge : 2 * edge, :] = speed[:edge, :]
        low_speed[1 : edge + 1, :] = speed[rows - edge :, :]
        from_pair = rows_first(pair[:rank] * pair[rank][None])
        from_other = rows_first(other[:rank] * other[rank][None])
        up_now[:edge] = jnp.where(even, from_other, from_pair)
        low_now[edge + 1 :] = jnp.where(even, from_pair, from_other)
        up_now[edge : edge + 2] = saved[0, :2]
        low_now[edge - 1 : edge + 1] = saved[0, 2:]
        a, b, c, d = up_now, up_prev, low_now, low_prev
        for step in range(1, STEPS + 1):
            advance_rows(step, edge + step, a, b, up_speed, step == 1)
            advance_rows(edge + 1 - step, 2 * edge + 1 - step, c, d, low_speed, step == 1)
            if step < STEPS:
                b[edge + step : edge + step + 2] = saved[step, :2]
                d[edge - 1 - step : edge + 1 - step] = saved[step, 2:]
            a, b, c, d = b, a, d, c
        for r in range(edge):
            upper = slice(r * cols, (r + 1) * cols)
            lower = slice(rim + r * cols, rim + (r + 1) * cols)
            inverse = 1.0 / speed[r : r + 1, :]
            out[0, :, upper] = a[edge + r] * inverse
            out[1, :, upper] = b[edge + r] * (-inverse)
            inverse = 1.0 / speed[rows - edge + r : rows - edge + r + 1, :]
            out[0, :, lower] = c[r + 1] * inverse
            out[1, :, lower] = d[r + 1] * (-inverse)

    short = pltpu.VMEM((2 * edge + 1, rank, cols), jnp.float32)
    short_speed = pltpu.VMEM((2 * edge + 1, cols), jnp.float32)
    rim_own = call(
        rim_kernel,
        f32(2, rank, 2 * rim),
        12,
        [short] * 4 + [short_speed] * 2,
        name="probes_rim",
    )(saved, courant, pair_halo, other_halo)
    rim_other = lax.ppermute(rim_own, "shot", to_other)

    def products(fields_ref, probes_ref, side, inside):
        total = jnp.zeros((2 * waves, 2 * rank), jnp.float32)
        places = [(rim, 0, inner * cols)] if inside else [(0, 0, rim), (cells - rim, rim, rim)]
        for level in range(2):
            for at, probe_at, count in places:
                pair = jnp.concatenate(parts_of(probes_ref[level, :, probe_at : probe_at + count], 2), 0)
                total = total + dot32(fields_ref[side, level, :, at : at + count], pair, NT)
        total = total[:waves] + total[waves:]
        return (total[:, :rank] + total[:, rank:]).T

    def product_kernel(fields_ref, inner_mine, inner_theirs, rim_mine, mine, theirs):
        side, _ = where_am_i()
        mine[...] = products(fields_ref, inner_mine, side, True) + products(
            fields_ref, rim_mine, side, False
        )
        theirs[...] = products(fields_ref, inner_theirs, 1 - side, True)

    def lay_out_raw(raw, blocks, out):
        for level in range(2):
            for first in range(0, waves, group):
                some = slice(first, first + group)
                low = slice(waves + first, waves + first + group)
                for place, block in enumerate(blocks):
                    for t in range(0, cols, LANES):
                        piece = raw[level, some, block : block + 8, t : t + LANES]
                        lay_out(piece, out.at[level], some, low, 8 * place, t)

    half = rank // 2

    def product_last_kernel(fields_ref, rim_theirs, mine_ref, theirs_ref, out):
        side, _ = where_am_i()
        mine = mine_ref[...]
        theirs = theirs_ref[...] + products(fields_ref, rim_theirs, 1 - side, False)
        for shot in range(shots):
            weights = jnp.where(side == shot, mine, theirs)
            weights = jnp.concatenate([weights[:half], weights[half:]], 1)
            for strip in range(strips):
                out[shot * strips + strip] = weights

    flops = 2 * 2 * waves * 2 * rank * cells * 2
    mine, theirs = call(product_kernel, [f32(rank, waves)] * 2, 24, name="product")(
        fields, inner_own, inner_other, rim_own
    )
    pieces = call(
        product_last_kernel, f32(shots * strips, half, 2 * waves), 24, name="product_last"
    )(fields, rim_other, mine, theirs)
    stage, pieces = lax.optimization_barrier((stage, pieces))
    raw = lax.ppermute(stage, "shot", to_other)
    pieces = lax.all_to_all(pieces, ("shot", "strip"), 0, 0)

    def combine(pieces_ref, fields_ref, swapped_ref, places, out):
        side, _ = where_am_i()
        weights = []
        for shot in range(shots):
            packed = jnp.sum(pieces_ref[shot * strips : (shot + 1) * strips], 0)
            weights.append(jnp.concatenate([packed[:, :waves], packed[:, waves:]], 0))
        stacks = []
        for own, other in (weights, weights[::-1]):
            stack = jnp.concatenate(parts_of(jnp.where(side == 0, own, other), 2), 0)
            stacks.append(jnp.concatenate([stack, stack], 1))
        for level in range(2):
            for at, place, count in places:
                both = jnp.dot(
                    stacks[0],
                    fields_ref[1 - side, level, :, at : at + count],
                    preferred_element_type=jnp.float32,
                ) + jnp.dot(
                    stacks[1],
                    swapped_ref[level, :, place : place + count],
                    preferred_element_type=jnp.float32,
                )
                out[level, :, place : place + count] = both[:rank] + both[rank:]

    def rim_terms_kernel(pieces_ref, fields_ref, raw, out, swapped):
        lay_out_raw(raw, [*range(0, edge, 8), *range(rows - edge, rows, 8)], swapped)
        places = [(0, 0, rim), (cells - rim, rim, rim)]
        combine(pieces_ref, fields_ref, swapped, places, out)

    def inner_terms_kernel(pieces_ref, fields_ref, raw, _, out, swapped):
        lay_out_raw(raw, range(edge, rows - edge, 8), swapped)
        combine(pieces_ref, fields_ref, swapped, [(rim, 0, inner * cols)], out)

    rim_terms = call(
        rim_terms_kernel,
        f32(2, rank, 2 * rim),
        24,
        [pltpu.VMEM((2, 2 * waves, 2 * rim), jnp.bfloat16)],
        name="terms_rim",
        flops=flops,
    )(pieces, fields, raw)

    def spill_kernel(
        own, speed, pair, other, pair_out, other_out,
        up_now, up_prev, low_now, low_prev, up_speed, low_speed,
    ):
        _, even = where_am_i()
        above, below = far_speeds(pair, other)
        up_speed[1 : edge + 1, :] = above
        up_speed[edge + 1 :, :] = speed[:edge, :]
        low_speed[:edge, :] = speed[rows - edge :, :]
        low_speed[edge : 2 * edge, :] = below
        zeros = jnp.zeros((edge + 1, rank, cols), jnp.float32)
        for up, low, level in ((up_now, low_now, 0), (up_prev, low_prev, 1)):
            up[: edge + 1] = zeros
            low[edge:] = zeros
            for r in range(edge):
                span = slice(r * cols, (r + 1) * cols)
                up[edge + 1 + r] = own[level, :, span]
                span = slice(rim + r * cols, rim + (r + 1) * cols)
                low[r] = own[level, :, span]
        a, b, c, d = up_now, up_prev, low_now, low_prev
        for step in range(1, STEPS + 1):
            advance_rows(edge + 1 - step, 2 * edge + 1 - step, a, b, up_speed, False)
            advance_rows(step, edge + step, c, d, low_speed, False)
            a, b, c, d = b, a, d, c
        pair_out[:, rim:] = jnp.zeros((rank, LANES), jnp.float32)
        for r in range(edge):
            span = slice(r * cols, (r + 1) * cols)
            upper, lower = a[1 + r], c[edge + r]
            pair_out[:, span] = jnp.where(even, lower, upper)
            other_out[:, span] = jnp.where(even, upper, lower)

    spill = f32(rank, rim)
    pair_spill, other_spill = call(
        spill_kernel,
        [f32(rank, rim + LANES), spill],
        16,
        [short] * 4 + [short_speed] * 2,
        name="spill",
    )(rim_terms, courant, pair_halo, other_halo)
    other_add = lax.ppermute(other_spill, "strip", to_next)
    pair_add = lax.ppermute(pair_spill, "strip", to_pair)

    inner_terms = call(
        inner_terms_kernel,
        f32(2, rank, inner * cols),
        24,
        [pltpu.VMEM((2, 2 * waves, inner * cols), jnp.bfloat16)],
        name="terms_inner",
        flops=flops,
    )(pieces, fields, raw, pair_spill)
    pad = STEPS // 2 + 1
    tall = rows + 2 * pad

    def sketch_kernel(
        rim_part, inner_part, speed, pair, other, _, out, now, prev, speeds
    ):
        above, below = far_speeds(pair, other)
        speeds[:pad, :] = above[edge - pad :, :]
        speeds[pad : pad + rows, :] = speed[...]
        speeds[pad + rows :, :] = below[:pad, :]
        zeros = jnp.zeros((pad, rank, cols), jnp.float32)
        for ref in (now, prev):
            ref[:pad] = zeros
            ref[pad + rows :] = zeros
        for r in range(rows):
            part, line = rim_part, r
            if edge <= r < rows - edge:
                part, line = inner_part, r - edge
            elif r >= edge:
                line = r - inner
            span = slice(line * cols, (line + 1) * cols)
            now[r + pad] = part[0, :, span]
            prev[r + pad] = part[1, :, span]
        a, b = now, prev
        for step in range(1, STEPS + 1):
            reach = min(step, STEPS - step)
            advance_rows(pad - reach, pad + rows + reach, a, b, speeds, False)
            a, b = b, a
        for r in range(rows):
            out[:, r * cols : (r + 1) * cols] = a[r + pad]

    lines = pltpu.VMEM((tall, rank, cols), jnp.float32)
    sketch_own = call(
        sketch_kernel,
        f32(rank, cells),
        16,
        [lines, lines, pltpu.VMEM((tall, cols), jnp.float32)],
        name="sketch",
        moved=8 * MIB,
    )(rim_terms, inner_terms, courant, pair_halo, other_halo, pair_spill)

    places = shots * strips

    def gram_kernel(own, pair, other, out, pieces_out):
        _, even = where_am_i()
        top = own[:, :rim] + jnp.where(even, other[:, :rim], pair[:, :rim])
        bottom = own[:, cells - rim :] + jnp.where(even, pair[:, :rim], other[:, :rim])
        middle = own[:, rim : cells - rim]
        out[:, :rim] = top
        out[:, rim : cells - rim] = middle
        out[:, cells - rim :] = bottom
        total = jnp.zeros((3 * rank, 3 * rank), jnp.float32)
        for piece in (top, middle, bottom):
            stack = jnp.concatenate(parts_of(piece, 3), 0)
            total = total + dot32(stack, stack, NT)
        wide = total[:, :rank] + total[:, rank : 2 * rank] + total[:, 2 * rank :]
        gram = wide[:rank] + wide[rank : 2 * rank] + wide[2 * rank :]
        gram = jnp.concatenate(
            [gram[:half], gram[half:], jnp.zeros((half, LANES - 2 * rank), jnp.float32)], 1
        )
        for place in range(places):
            pieces_out[place] = gram

    sketch, gram_pieces = call(
        gram_kernel, [f32(rank, cells), f32(places, rank // 2, LANES)], 12, name="gram"
    )(sketch_own, pair_add, other_add)
    sketch_other = lax.ppermute(sketch, "shot", to_other)
    gram_pieces = lax.all_to_all(gram_pieces, ("shot", "strip"), 0, 0)

    def factor_kernel(grams, own, theirs, left_out, right_out, held, sems):
        side, _ = where_am_i()
        line = lax.broadcasted_iota(jnp.int32, (rank, rank), 0)
        column = lax.broadcasted_iota(jnp.int32, (rank, rank), 1)
        tall_line = lax.broadcasted_iota(jnp.int32, (rank, LANES), 0)
        sides = []
        for shot in range(2):
            halves = jnp.sum(grams[shot * strips : (shot + 1) * strips], 0)
            gram = jnp.concatenate([halves[:, :rank], halves[:, rank : 2 * rank]], 0)
            columns = [jnp.broadcast_to(gram[:, j : j + 1], (rank, LANES)) for j in range(rank)]
            sides.append((columns, [jnp.where(line == column, 1.0, 0.0)]))
        for j in range(rank):
            for columns, inverse in sides:
                factor = columns[j] * (1.0 / columns[j][j : j + 1])
                factor = jnp.where(tall_line > j, factor, 0.0)
                for k in range(j + 1, rank):
                    columns[k] = columns[k] - factor * columns[k][j : j + 1]
                inverse[0] = inverse[0] - factor[:, :rank] * inverse[0][j : j + 1]
        copies = []
        for (columns, inverse), shot, out in zip(sides, (0, 1), (left_out, right_out)):
            pivots = columns[0]
            for j in range(1, rank):
                pivots = jnp.where(tall_line == j, columns[j], pivots)
            inverse = inverse[0] * (lax.rsqrt(pivots[:, :rank]) * factor_scale)
            stack = jnp.concatenate(parts_of(inverse, 3), 0)
            stack = jnp.concatenate([stack] * 3, 1)
            for block in range(0, rows, 8):
                span = slice(block * cols, (block + 8) * cols)
                lines = jnp.where(side == shot, own[:, span], theirs[:, span])
                thick = jnp.concatenate(parts_of(lines, 3), 0)
                solved = jnp.dot(stack, thick, preferred_element_type=jnp.float32)
                solved = solved[:rank] + solved[rank : 2 * rank] + solved[2 * rank :]
                for t in range(0, cols, LANES):
                    tile = [solved[:, r * cols + t : r * cols + t + LANES][None] for r in range(8)]
                    held[shot, :, block : block + 8, t : t + LANES] = jnp.swapaxes(
                        jnp.concatenate(tile, 0), 0, 1
                    )
                lines_here = pl.ds(block, 8)
                copies.append(
                    pltpu.make_async_copy(
                        held.at[shot, :, lines_here], out.at[:, lines_here], sems.at[shot, block // 8]
                    )
                )
                copies[-1].start()
        for copy in copies:
            copy.wait()

    factor = f32(rank, rows, cols)
    left_factor, right_factor = pl.pallas_call(
        factor_kernel,
        out_shape=[factor, factor],
        in_specs=[near] * 3,
        out_specs=[far] * 2,
        scratch_shapes=[
            pltpu.VMEM((2, rank, rows, cols), jnp.float32),
            pltpu.SemaphoreType.DMA((2, rows // 8)),
        ],
        compiler_params=pltpu.CompilerParams(vmem_limit_bytes=12 * MIB),
        name="factors",
    )(gram_pieces, sketch, sketch_other)
    return left_factor, right_factor


def solution(mesh):
    return jax.shard_map(
        shards,
        mesh=mesh,
        in_specs=(
            P("shot", None, "strip", None),
            P("shot", None, "strip", None),
            P("shot", None, "strip", None),
            P("shot", None, "strip", None),
            P("strip", None),
            P(None, "strip", None),
            P(None, "strip", None),
        ),
        out_specs=(P(None, "strip", None), P(None, "strip", None)),
        check_vma=False,
    )
```

```python
import math

import jax
import jax.numpy as jnp
from jax import lax
from jax.experimental import pallas as pl
from jax.experimental.pallas import tpu as pltpu
from jax.sharding import PartitionSpec as P

STEPS = 8
LANES = 128
NT = (((1,), (1,)), ((), ()))
MIB = 1 << 20


def in_hbm(x):
    return pltpu.with_memory_space_constraint(x, pltpu.HBM)


def parts_of(x, count):
    parts = []
    for index in range(count):
        part = x.astype(jnp.bfloat16)
        parts.append(part)
        if index + 1 < count:
            x = x - part.astype(jnp.float32)
    return parts


def dot32(a, b, dims):
    return lax.dot_general(a, b, dims, preferred_element_type=jnp.float32)


def call(kernel, outs, vmem_mib, scratch=(), name=None, flops=0, moved=0):
    many = isinstance(outs, (list, tuple))
    spec = pl.BlockSpec(memory_space=pltpu.VMEM)
    return pl.pallas_call(
        kernel,
        out_shape=outs,
        out_specs=[spec] * len(outs) if many else spec,
        scratch_shapes=list(scratch),
        compiler_params=pltpu.CompilerParams(vmem_limit_bytes=vmem_mib * MIB),
        cost_estimate=pl.CostEstimate(flops=flops, bytes_accessed=moved, transcendentals=0),
        name=name,
    )


def f32(*shape):
    return jax.ShapeDtypeStruct(shape, jnp.float32)


def rows_first(x):
    return jnp.concatenate(
        [jnp.swapaxes(x[:, :, t : t + LANES], 0, 1) for t in range(0, x.shape[2], LANES)], 2
    )


def advance_rows(first, last, now, prev, speed, fresh):
    tiles = now.shape[2] // LANES
    spans = [slice(t * LANES, (t + 1) * LANES) for t in range(tiles)]
    lane = lax.broadcasted_iota(jnp.int32, (now.shape[1], LANES), 1)
    at_start, at_end = lane == 0, lane == LANES - 1
    above = [now[first - 1, :, span] for span in spans]
    centre = [now[first, :, span] for span in spans]
    for r in range(first, last):
        below = [now[r + 1, :, span] for span in spans]
        from_left = [pltpu.roll(c, 1, 1) for c in centre]
        from_right = [pltpu.roll(c, LANES - 1, 1) for c in centre]
        for t, span in enumerate(spans):
            left = jnp.where(at_start, from_left[t - 1] if t else 0.0, from_left[t])
            right = jnp.where(at_end, from_right[t + 1] if t + 1 < tiles else 0.0, from_right[t])
            c = speed[r : r + 1, span]
            around = (above[t] + below[t]) + (left + right)
            value = (2.0 - 4.0 * c) * centre[t] + c * around
            if not fresh:
                value = value - prev[r, :, span]
            prev[r, :, span] = value
        above, centre = centre, below


def shards(source_now, source_prev, adjoint_now, adjoint_prev, courant, probe_left, probe_right):
    _, waves, rows, cols = source_now.shape
    rank = probe_left.shape[0]
    strips, shots = lax.axis_size("strip"), lax.axis_size("shot")
    cells = rows * cols
    edge = STEPS
    factor_scale = math.sqrt(cells * strips)

    to_other = [(0, 1), (1, 0)]
    to_pair = [(i, i ^ 1) for i in range(strips)]
    to_next = [(i, i + 1) for i in range(1, strips - 1, 2)]
    to_next = to_next + [(b, a) for a, b in to_next]

    def where_am_i():
        return lax.axis_index("shot"), lax.rem(lax.axis_index("strip"), 2) == 0

    def edges_kernel(left, right, speed, pair, other, sem):
        side, even = where_am_i()
        pair_row = jnp.where(even, rows - edge, 0)
        other_row = jnp.where(even, 0, rows - edge)

        def copies(probe):
            made = []
            for index, (out, start) in enumerate(((pair, pair_row), (other, other_row))):
                start = pl.multiple_of(start, 8)
                if out.shape[0] > rank + 1:
                    made.append(
                        pltpu.make_async_copy(speed.at[pl.ds(start, edge), :], out.at[rank + 1], sem.at[4])
                    )
                made.append(
                    pltpu.make_async_copy(
                        probe.at[:, pl.ds(start, edge), :], out.at[pl.ds(0, rank)], sem.at[2 * index]
                    )
                )
                made.append(
                    pltpu.make_async_copy(
                        speed.at[pl.ds(start, edge), :], out.at[rank], sem.at[2 * index + 1]
                    )
                )
            for copy in made:
                copy.start()
            for copy in made:
                copy.wait()

        @pl.when(side == 0)
        def _():
            copies(left)

        @pl.when(side != 0)
        def _():
            copies(right)

    halo = f32(rank + 1, edge, cols)
    far = pl.BlockSpec(memory_space=pltpu.HBM)
    near = pl.BlockSpec(memory_space=pltpu.VMEM)
    pair_edge, other_edge = pl.pallas_call(
        edges_kernel,
        out_shape=[f32(rank + 2, edge, cols), halo],
        in_specs=[far] * 3,
        out_specs=[near] * 2,
        scratch_shapes=[pltpu.SemaphoreType.DMA((5,))],
        compiler_params=pltpu.CompilerParams(vmem_limit_bytes=4 * MIB),
        cost_estimate=pl.CostEstimate(flops=20000000000, bytes_accessed=4194304, transcendentals=0),
        name="edges",
    )(in_hbm(probe_left), in_hbm(probe_right), in_hbm(courant))
    other_halo = lax.ppermute(other_edge, "strip", to_next)
    pair_halo = lax.ppermute(pair_edge, "strip", to_pair)

    group = math.gcd(waves, 16)

    def lay_out(lines, out, high_at, low_at, at, t):
        high, low = parts_of(lines, 2)
        for r in range(8):
            span = slice((at + r) * cols + t, (at + r) * cols + t + LANES)
            out[high_at, span] = high[r]
            out[low_at, span] = low[r]

    def split_kernel(
        adjoint_a, adjoint_b, source_a, source_b, left, right, speeds, _,
        out, start, stage, probe, speed, sem,
    ):
        side, _ = where_am_i()

        def probe_copy(ref):
            return pltpu.make_async_copy(ref, probe, sem.at[0])

        speed_copy = pltpu.make_async_copy(speeds, speed, sem.at[1])
        speed_copy.start()

        @pl.when(side == 0)
        def _():
            probe_copy(left).start()

        @pl.when(side != 0)
        def _():
            probe_copy(right).start()

        for level, adjoint, source in ((0, adjoint_a, source_a), (1, adjoint_b, source_b)):
            for first in range(0, waves, group):
                some = slice(first, first + group)
                low = slice(waves + first, waves + first + group)
                for block in range(0, rows, 8):
                    for t in range(0, cols, LANES):
                        span = slice(t, t + LANES)
                        mine = jnp.swapaxes(adjoint[some, block : block + 8, span], 0, 1)
                        other = jnp.swapaxes(source[some, block : block + 8, span], 0, 1)
                        stage[level, block : block + 8, some, span] = jnp.where(side == 0, mine, other)
                        lay_out(mine, out.at[0, level], some, low, block, t)
                        lay_out(other, out.at[1, level], some, low, block, t)
        speed_copy.wait()
        probe_copy(left).wait()
        for block in range(0, rows, 8):
            span = slice(block, block + 8)
            start[span] = rows_first(probe[:, span, :]) * speed[span, :][:, None, :]

    fields, start, stage = pl.pallas_call(
        split_kernel,
        out_shape=[
            jax.ShapeDtypeStruct((2, 2, 2 * waves, cells), jnp.bfloat16),
            f32(rows, rank, cols),
            f32(2, rows, waves, cols),
        ],
        in_specs=[near] * 4 + [far] * 3 + [pl.BlockSpec(memory_space=pl.ANY)],
        out_specs=[near] * 3,
        scratch_shapes=[
            pltpu.VMEM((rank, rows, cols), jnp.float32),
            pltpu.VMEM((rows, cols), jnp.float32),
            pltpu.SemaphoreType.DMA((2,)),
        ],
        compiler_params=pltpu.CompilerParams(vmem_limit_bytes=26 * MIB),
        cost_estimate=pl.CostEstimate(flops=0, bytes_accessed=16 * waves * cells * 2, transcendentals=0),
        name="split",
    )(
        adjoint_now[0], adjoint_prev[0], source_now[0], source_prev[0],
        *map(in_hbm, (probe_left, probe_right, courant)),
        pair_edge,
    )
    inner = rows - 2 * edge
    rim = edge * cols

    def inner_kernel(begin, speed, out, saved, now, prev):
        now[...] = begin[...]
        a, b = now, prev
        for step in range(STEPS):
            saved[step, :2] = a[step : step + 2]
            saved[step, 2:] = a[rows - 2 - step : rows - step]
            advance_rows(step + 1, rows - 1 - step, a, b, speed, step == 0)
            a, b = b, a
        for r in range(edge, edge + inner):
            span = slice((r - edge) * cols, (r - edge + 1) * cols)
            inverse = 1.0 / speed[r : r + 1, :]
            out[0, :, span] = a[r] * inverse
            out[1, :, span] = b[r] * (-inverse)

    state = pltpu.VMEM((rows, rank, cols), jnp.float32)
    inner_own, saved = call(
        inner_kernel,
        [f32(2, rank, inner * cols), f32(STEPS, 4, rank, cols)],
        12,
        [state, state],
        name="probes_inner",
    )(start, courant)
    inner_other = lax.ppermute(inner_own, "shot", to_other)

    def far_speeds(pair, other):
        _, even = where_am_i()
        above = jnp.where(even, other[rank], pair[rank])
        below = jnp.where(even, pair[rank], other[rank])
        return above, below

    def rim_kernel(saved, speed, pair, other, out, up_now, up_prev, low_now, low_prev, up_speed, low_speed):
        _, even = where_am_i()
        up_speed[:edge, :], low_speed[edge + 1 :, :] = far_speeds(pair, other)
        up_speed[edge : 2 * edge, :] = speed[:edge, :]
        low_speed[1 : edge + 1, :] = speed[rows - edge :, :]
        from_pair = rows_first(pair[:rank] * pair[rank][None])
        from_other = rows_first(other[:rank] * other[rank][None])
        up_now[:edge] = jnp.where(even, from_other, from_pair)
        low_now[edge + 1 :] = jnp.where(even, from_pair, from_other)
        up_now[edge : edge + 2] = saved[0, :2]
        low_now[edge - 1 : edge + 1] = saved[0, 2:]
        a, b, c, d = up_now, up_prev, low_now, low_prev
        for step in range(1, STEPS + 1):
            advance_rows(step, edge + step, a, b, up_speed, step == 1)
            advance_rows(edge + 1 - step, 2 * edge + 1 - step, c, d, low_speed, step == 1)
            if step < STEPS:
                b[edge + step : edge + step + 2] = saved[step, :2]
                d[edge - 1 - step : edge + 1 - step] = saved[step, 2:]
            a, b, c, d = b, a, d, c
        for r in range(edge):
            upper = slice(r * cols, (r + 1) * cols)
            lower = slice(rim + r * cols, rim + (r + 1) * cols)
            inverse = 1.0 / speed[r : r + 1, :]
            out[0, :, upper] = a[edge + r] * inverse
            out[1, :, upper] = b[edge + r] * (-inverse)
            inverse = 1.0 / speed[rows - edge + r : rows - edge + r + 1, :]
            out[0, :, lower] = c[r + 1] * inverse
            out[1, :, lower] = d[r + 1] * (-inverse)

    short = pltpu.VMEM((2 * edge + 1, rank, cols), jnp.float32)
    short_speed = pltpu.VMEM((2 * edge + 1, cols), jnp.float32)
    rim_own = call(
        rim_kernel,
        f32(2, rank, 2 * rim),
        12,
        [short] * 4 + [short_speed] * 2,
        name="probes_rim",
    )(saved, courant, pair_halo, other_halo)
    rim_other = lax.ppermute(rim_own, "shot", to_other)

    def products(fields_ref, probes_ref, side, inside):
        total = jnp.zeros((2 * waves, 2 * rank), jnp.float32)
        places = [(rim, 0, inner * cols)] if inside else [(0, 0, rim), (cells - rim, rim, rim)]
        for level in range(2):
            for at, probe_at, count in places:
                pair = jnp.concatenate(parts_of(probes_ref[level, :, probe_at : probe_at + count], 2), 0)
                total = total + dot32(fields_ref[side, level, :, at : at + count], pair, NT)
        total = total[:waves] + total[waves:]
        return (total[:, :rank] + total[:, rank:]).T

    def product_kernel(fields_ref, inner_mine, inner_theirs, rim_mine, mine, theirs):
        side, _ = where_am_i()
        mine[...] = products(fields_ref, inner_mine, side, True) + products(
            fields_ref, rim_mine, side, False
        )
        theirs[...] = products(fields_ref, inner_theirs, 1 - side, True)

    half = rank // 2

    def product_last_kernel(fields_ref, rim_theirs, mine_ref, theirs_ref, out):
        side, _ = where_am_i()
        mine = mine_ref[...]
        theirs = theirs_ref[...] + products(fields_ref, rim_theirs, 1 - side, False)
        for shot in range(shots):
            weights = jnp.where(side == shot, mine, theirs)
            weights = jnp.concatenate([weights[:half], weights[half:]], 1)
            for strip in range(strips):
                out[shot * strips + strip] = weights

    flops = 2 * 2 * waves * 2 * rank * cells * 2
    mine, theirs = call(product_kernel, [f32(rank, waves)] * 2, 24, name="product")(
        fields, inner_own, inner_other, rim_own
    )
    pieces = call(
        product_last_kernel, f32(shots * strips, half, 2 * waves), 24, name="product_last"
    )(fields, rim_other, mine, theirs)
    stage, pieces = lax.optimization_barrier((stage, pieces))
    raw = lax.ppermute(stage, "shot", to_other)
    pieces = lax.all_to_all(pieces, ("shot", "strip"), 0, 0)

    def combine(pieces_ref, fields_ref, raw, blocks, out, swapped):
        side, _ = where_am_i()
        weights = []
        for shot in range(shots):
            packed = jnp.sum(pieces_ref[shot * strips : (shot + 1) * strips], 0)
            weights.append(jnp.concatenate([packed[:, :waves], packed[:, waves:]], 0))
        stacks = []
        for own, other in (weights, weights[::-1]):
            stack = jnp.concatenate(parts_of(jnp.where(side == 0, own, other), 2), 0)
            stacks.append(jnp.concatenate([stack, stack], 1))
        for level in range(2):
            for place, block in enumerate(blocks):
                here = slice(block * cols, (block + 8) * cols)
                there = slice(place * 8 * cols, (place + 1) * 8 * cols)
                for r in range(8):
                    high, low = parts_of(raw[level, block + r], 2)
                    span = slice((place * 8 + r) * cols, (place * 8 + r + 1) * cols)
                    swapped[level, :waves, span] = high
                    swapped[level, waves:, span] = low
                both = jnp.dot(
                    stacks[0], fields_ref[1 - side, level, :, here], preferred_element_type=jnp.float32
                ) + jnp.dot(stacks[1], swapped[level, :, there], preferred_element_type=jnp.float32)
                out[level, :, there] = both[:rank] + both[rank:]

    def rim_terms_kernel(pieces_ref, fields_ref, raw, out, swapped):
        blocks = [*range(0, edge, 8), *range(rows - edge, rows, 8)]
        combine(pieces_ref, fields_ref, raw, blocks, out, swapped)

    def inner_terms_kernel(pieces_ref, fields_ref, raw, _, out, swapped):
        combine(pieces_ref, fields_ref, raw, range(edge, rows - edge, 8), out, swapped)

    rim_terms = call(
        rim_terms_kernel,
        f32(2, rank, 2 * rim),
        24,
        [pltpu.VMEM((2, 2 * waves, 2 * rim), jnp.bfloat16)],
        name="terms_rim",
        flops=flops,
    )(pieces, fields, raw)

    def spill_kernel(
        own, speed, pair, other, pair_out, other_out, saved,
        up_now, up_prev, low_now, low_prev, up_speed, low_speed,
    ):
        _, even = where_am_i()
        above, below = far_speeds(pair, other)
        up_speed[1 : edge + 1, :] = above
        up_speed[edge + 1 :, :] = speed[:edge, :]
        low_speed[:edge, :] = speed[rows - edge :, :]
        low_speed[edge : 2 * edge, :] = below
        zeros = jnp.zeros((edge + 1, rank, cols), jnp.float32)
        for up, low, level in ((up_now, low_now, 0), (up_prev, low_prev, 1)):
            up[: edge + 1] = zeros
            low[edge:] = zeros
            for r in range(edge):
                span = slice(r * cols, (r + 1) * cols)
                up[edge + 1 + r] = own[level, :, span]
                span = slice(rim + r * cols, rim + (r + 1) * cols)
                low[r] = own[level, :, span]
        a, b, c, d = up_now, up_prev, low_now, low_prev
        for step in range(1, STEPS + 1):
            advance_rows(edge + 1 - step, 2 * edge + 1 - step, a, b, up_speed, False)
            advance_rows(step, edge + step, c, d, low_speed, False)
            if step < STEPS:
                saved[step - 1, :2] = b[2 * edge - 1 - step : 2 * edge + 1 - step]
                saved[step - 1, 2:] = d[step : step + 2]
            a, b, c, d = b, a, d, c
        pair_out[:, rim:] = jnp.zeros((rank, LANES), jnp.float32)
        for r in range(edge):
            span = slice(r * cols, (r + 1) * cols)
            upper, lower = a[1 + r], c[edge + r]
            pair_out[:, span] = jnp.where(even, lower, upper)
            other_out[:, span] = jnp.where(even, upper, lower)

    spill = f32(rank, rim)
    pair_spill, other_spill, spill_saved = call(
        spill_kernel,
        [f32(rank, rim + LANES), spill, f32(STEPS - 1, 4, rank, cols)],
        16,
        [short] * 4 + [short_speed] * 2,
        name="spill",
    )(rim_terms, courant, pair_halo, other_halo)
    other_add = lax.ppermute(other_spill, "strip", to_next)
    pair_add = lax.ppermute(pair_spill, "strip", to_pair)

    inner_terms = call(
        inner_terms_kernel,
        f32(2, rank, inner * cols),
        24,
        [pltpu.VMEM((2, 2 * waves, inner * cols), jnp.bfloat16)],
        name="terms_inner",
        flops=flops,
    )(pieces, fields, raw, pair_spill)
    def gram_of(piece):
        stack = jnp.concatenate(parts_of(piece, 3), 0)
        return dot32(stack, stack, NT)

    def sketch_kernel(rim_part, inner_part, speed, saved, out, gram_out, now, prev, speeds):
        speeds[1 : rows + 1, :] = speed[...]
        for r in range(edge - 2, rows - edge + 2):
            part, line = rim_part, r
            if edge <= r < rows - edge:
                part, line = inner_part, r - edge
            elif r >= edge:
                line = r - inner
            span = slice(line * cols, (line + 1) * cols)
            now[r + 1] = part[0, :, span]
            prev[r + 1] = part[1, :, span]
        a, b = now, prev
        for step in range(1, STEPS + 1):
            first, last = edge + 1 - step, rows - edge + 1 + step
            advance_rows(first, last, a, b, speeds, False)
            if step < STEPS:
                b[first - 2 : first] = saved[step - 1, :2]
                b[last : last + 2] = saved[step - 1, 2:]
            a, b = b, a
        for r in range(rows):
            out[:, r * cols : (r + 1) * cols] = a[r + 1]
        gram_out[...] = gram_of(out[:, rim : cells - rim])

    lines = pltpu.VMEM((rows + 2, rank, cols), jnp.float32)
    sketch_own, inner_gram = call(
        sketch_kernel,
        [f32(rank, cells), f32(3 * rank, 3 * rank)],
        16,
        [lines, lines, pltpu.VMEM((rows + 2, cols), jnp.float32)],
        name="sketch",
        moved=8 * MIB,
    )(rim_terms, inner_terms, courant, spill_saved)

    places = shots * strips

    def gram_kernel(own, pair, other, inner_total, out, pieces_out):
        _, even = where_am_i()
        top = own[:, :rim] + jnp.where(even, other[:, :rim], pair[:, :rim])
        bottom = own[:, cells - rim :] + jnp.where(even, pair[:, :rim], other[:, :rim])
        out[:, :rim] = top
        out[:, cells - rim :] = bottom
        total = inner_total[...] + gram_of(jnp.concatenate([top, bottom], 1))
        wide = total[:, :rank] + total[:, rank : 2 * rank] + total[:, 2 * rank :]
        gram = wide[:rank] + wide[rank : 2 * rank] + wide[2 * rank :]
        gram = jnp.concatenate(
            [gram[:half], gram[half:], jnp.zeros((half, LANES - 2 * rank), jnp.float32)], 1
        )
        for place in range(places):
            pieces_out[place] = gram

    sketch, gram_pieces = pl.pallas_call(
        gram_kernel,
        out_shape=[f32(rank, cells), f32(places, rank // 2, LANES)],
        in_specs=[near] * 4,
        out_specs=[near] * 2,
        input_output_aliases={0: 0},
        compiler_params=pltpu.CompilerParams(vmem_limit_bytes=12 * MIB),
        name="gram",
    )(sketch_own, pair_add, other_add, inner_gram)
    sketch_other = lax.ppermute(sketch, "shot", to_other)
    gram_pieces = lax.all_to_all(gram_pieces, ("shot", "strip"), 0, 0)

    def factor_kernel(grams, own, theirs, left_out, right_out, held, thick, sems):
        side, _ = where_am_i()
        for shot in range(2):
            for block in range(0, rows, 8):
                span = slice(block * cols, (block + 8) * cols)
                lines = jnp.where(side == shot, own[:, span], theirs[:, span])
                thick[shot, :, span] = jnp.concatenate(parts_of(lines, 3), 0)
        line = lax.broadcasted_iota(jnp.int32, (rank, rank), 0)
        column = lax.broadcasted_iota(jnp.int32, (rank, rank), 1)
        tall_line = lax.broadcasted_iota(jnp.int32, (rank, LANES), 0)
        sides = []
        for shot in range(2):
            halves = jnp.sum(grams[shot * strips : (shot + 1) * strips], 0)
            gram = jnp.concatenate([halves[:, :rank], halves[:, rank : 2 * rank]], 0)
            columns = [jnp.broadcast_to(gram[:, j : j + 1], (rank, LANES)) for j in range(rank)]
            sides.append((columns, [jnp.where(line == column, 1.0, 0.0)]))
        for j in range(rank):
            for columns, inverse in sides:
                factor = columns[j] * (1.0 / columns[j][j : j + 1])
                factor = jnp.where(tall_line > j, factor, 0.0)
                for k in range(j + 1, rank):
                    columns[k] = columns[k] - factor * columns[k][j : j + 1]
                inverse[0] = inverse[0] - factor[:, :rank] * inverse[0][j : j + 1]
        copies = []
        for (columns, inverse), shot, out in zip(sides, (0, 1), (left_out, right_out)):
            pivots = columns[0]
            for j in range(1, rank):
                pivots = jnp.where(tall_line == j, columns[j], pivots)
            inverse = inverse[0] * (lax.rsqrt(pivots[:, :rank]) * factor_scale)
            stack = jnp.concatenate(parts_of(inverse, 3), 0)
            stack = jnp.concatenate([stack] * 3, 1)
            for block in range(0, rows, 8):
                span = slice(block * cols, (block + 8) * cols)
                solved = jnp.dot(stack, thick[shot, :, span], preferred_element_type=jnp.float32)
                solved = solved[:rank] + solved[rank : 2 * rank] + solved[2 * rank :]
                for t in range(0, cols, LANES):
                    tile = [solved[:, r * cols + t : r * cols + t + LANES][None] for r in range(8)]
                    held[shot, :, block : block + 8, t : t + LANES] = jnp.swapaxes(
                        jnp.concatenate(tile, 0), 0, 1
                    )
                lines_here = pl.ds(block, 8)
                copies.append(
                    pltpu.make_async_copy(
                        held.at[shot, :, lines_here], out.at[:, lines_here], sems.at[shot, block // 8]
                    )
                )
                copies[-1].start()
        for copy in copies:
            copy.wait()

    factor = f32(rank, rows, cols)
    left_factor, right_factor = pl.pallas_call(
        factor_kernel,
        out_shape=[factor, factor],
        in_specs=[near] * 3,
        out_specs=[far] * 2,
        scratch_shapes=[
            pltpu.VMEM((2, rank, rows, cols), jnp.float32),
            pltpu.VMEM((2, 3 * rank, cells), jnp.bfloat16),
            pltpu.SemaphoreType.DMA((2, rows // 8)),
        ],
        compiler_params=pltpu.CompilerParams(vmem_limit_bytes=12 * MIB),
        name="factors",
    )(gram_pieces, sketch, sketch_other)
    return left_factor, right_factor


def solution(mesh):
    return jax.shard_map(
        shards,
        mesh=mesh,
        in_specs=(
            P("shot", None, "strip", None),
            P("shot", None, "strip", None),
            P("shot", None, "strip", None),
            P("shot", None, "strip", None),
            P("strip", None),
            P(None, "strip", None),
            P(None, "strip", None),
        ),
        out_specs=(P(None, "strip", None), P(None, "strip", None)),
        check_vma=False,
    )
```

```python
import math

import jax
import jax.numpy as jnp
from jax import lax
from jax.experimental import pallas as pl
from jax.experimental.pallas import tpu as pltpu
from jax.sharding import PartitionSpec as P

STEPS = 8
LANES = 128
NT = (((1,), (1,)), ((), ()))
MIB = 1 << 20


def in_hbm(x):
    return pltpu.with_memory_space_constraint(x, pltpu.HBM)


def parts_of(x, count):
    parts = []
    for index in range(count):
        part = x.astype(jnp.bfloat16)
        parts.append(part)
        if index + 1 < count:
            x = x - part.astype(jnp.float32)
    return parts


def dot32(a, b, dims):
    return lax.dot_general(a, b, dims, preferred_element_type=jnp.float32)


def call(kernel, outs, vmem_mib, scratch=(), name=None, flops=0, moved=0):
    many = isinstance(outs, (list, tuple))
    spec = pl.BlockSpec(memory_space=pltpu.VMEM)
    return pl.pallas_call(
        kernel,
        out_shape=outs,
        out_specs=[spec] * len(outs) if many else spec,
        scratch_shapes=list(scratch),
        compiler_params=pltpu.CompilerParams(vmem_limit_bytes=vmem_mib * MIB),
        cost_estimate=pl.CostEstimate(flops=flops, bytes_accessed=moved, transcendentals=0),
        name=name,
    )


def f32(*shape):
    return jax.ShapeDtypeStruct(shape, jnp.float32)


def rows_first(x):
    return jnp.concatenate(
        [jnp.swapaxes(x[:, :, t : t + LANES], 0, 1) for t in range(0, x.shape[2], LANES)], 2
    )


def advance_rows(first, last, now, prev, speed, fresh):
    tiles = now.shape[2] // LANES
    spans = [slice(t * LANES, (t + 1) * LANES) for t in range(tiles)]
    lane = lax.broadcasted_iota(jnp.int32, (now.shape[1], LANES), 1)
    at_start, at_end = lane == 0, lane == LANES - 1
    above = [now[first - 1, :, span] for span in spans]
    centre = [now[first, :, span] for span in spans]
    for r in range(first, last):
        below = [now[r + 1, :, span] for span in spans]
        from_left = [pltpu.roll(c, 1, 1) for c in centre]
        from_right = [pltpu.roll(c, LANES - 1, 1) for c in centre]
        for t, span in enumerate(spans):
            left = jnp.where(at_start, from_left[t - 1] if t else 0.0, from_left[t])
            right = jnp.where(at_end, from_right[t + 1] if t + 1 < tiles else 0.0, from_right[t])
            c = speed[r : r + 1, span]
            around = (above[t] + below[t]) + (left + right)
            value = (2.0 - 4.0 * c) * centre[t] + c * around
            if not fresh:
                value = value - prev[r, :, span]
            prev[r, :, span] = value
        above, centre = centre, below


def shards(source_now, source_prev, adjoint_now, adjoint_prev, courant, probe_left, probe_right):
    _, waves, rows, cols = source_now.shape
    rank = probe_left.shape[0]
    strips, shots = lax.axis_size("strip"), lax.axis_size("shot")
    cells = rows * cols
    edge = STEPS
    factor_scale = math.sqrt(cells * strips)

    to_other = [(0, 1), (1, 0)]
    to_pair = [(i, i ^ 1) for i in range(strips)]
    to_next = [(i, i + 1) for i in range(1, strips - 1, 2)]
    to_next = to_next + [(b, a) for a, b in to_next]

    def where_am_i():
        return lax.axis_index("shot"), lax.rem(lax.axis_index("strip"), 2) == 0

    def edges_kernel(left, right, speed, pair, other, sem):
        side, even = where_am_i()
        pair_row = jnp.where(even, rows - edge, 0)
        other_row = jnp.where(even, 0, rows - edge)

        def copies(probe):
            made = []
            for index, (out, start) in enumerate(((pair, pair_row), (other, other_row))):
                start = pl.multiple_of(start, 8)
                if out.shape[0] > rank + 1:
                    made.append(
                        pltpu.make_async_copy(speed.at[pl.ds(start, edge), :], out.at[rank + 1], sem.at[4])
                    )
                made.append(
                    pltpu.make_async_copy(
                        probe.at[:, pl.ds(start, edge), :], out.at[pl.ds(0, rank)], sem.at[2 * index]
                    )
                )
                made.append(
                    pltpu.make_async_copy(
                        speed.at[pl.ds(start, edge), :], out.at[rank], sem.at[2 * index + 1]
                    )
                )
            for copy in made:
                copy.start()
            for copy in made:
                copy.wait()

        @pl.when(side == 0)
        def _():
            copies(left)

        @pl.when(side != 0)
        def _():
            copies(right)

    halo = f32(rank + 1, edge, cols)
    far = pl.BlockSpec(memory_space=pltpu.HBM)
    near = pl.BlockSpec(memory_space=pltpu.VMEM)
    pair_edge, other_edge = pl.pallas_call(
        edges_kernel,
        out_shape=[f32(rank + 2, edge, cols), halo],
        in_specs=[far] * 3,
        out_specs=[near] * 2,
        scratch_shapes=[pltpu.SemaphoreType.DMA((5,))],
        compiler_params=pltpu.CompilerParams(vmem_limit_bytes=4 * MIB),
        cost_estimate=pl.CostEstimate(flops=20000000000, bytes_accessed=4194304, transcendentals=0),
        name="edges",
    )(in_hbm(probe_left), in_hbm(probe_right), in_hbm(courant))
    other_halo = lax.ppermute(other_edge, "strip", to_next)
    pair_halo = lax.ppermute(pair_edge, "strip", to_pair)

    group = math.gcd(waves, 16)

    def lay_out(lines, out, high_at, low_at, at, t):
        high, low = parts_of(lines, 2)
        for r in range(8):
            span = slice((at + r) * cols + t, (at + r) * cols + t + LANES)
            out[high_at, span] = high[r]
            out[low_at, span] = low[r]

    def split_kernel(
        adjoint_a, adjoint_b, source_a, source_b, left, right, speeds, _,
        out, start, stage, probe, speed, sem,
    ):
        side, _ = where_am_i()

        def probe_copy(ref):
            return pltpu.make_async_copy(ref, probe, sem.at[0])

        speed_copy = pltpu.make_async_copy(speeds, speed, sem.at[1])
        speed_copy.start()

        @pl.when(side == 0)
        def _():
            probe_copy(left).start()

        @pl.when(side != 0)
        def _():
            probe_copy(right).start()

        for level, adjoint, source in ((0, adjoint_a, source_a), (1, adjoint_b, source_b)):
            for first in range(0, waves, group):
                some = slice(first, first + group)
                low = slice(waves + first, waves + first + group)
                for block in range(0, rows, 8):
                    for t in range(0, cols, LANES):
                        span = slice(t, t + LANES)
                        mine = jnp.swapaxes(adjoint[some, block : block + 8, span], 0, 1)
                        other = jnp.swapaxes(source[some, block : block + 8, span], 0, 1)
                        stage[level, block : block + 8, some, span] = jnp.where(side == 0, mine, other)
                        lay_out(mine, out.at[0, level], some, low, block, t)
                        lay_out(other, out.at[1, level], some, low, block, t)
        speed_copy.wait()
        probe_copy(left).wait()
        for block in range(0, rows, 8):
            span = slice(block, block + 8)
            start[span] = rows_first(probe[:, span, :]) * speed[span, :][:, None, :]

    fields, start, stage = pl.pallas_call(
        split_kernel,
        out_shape=[
            jax.ShapeDtypeStruct((2, 2, 2 * waves, cells), jnp.bfloat16),
            f32(rows, rank, cols),
            f32(2, rows, waves, cols),
        ],
        in_specs=[near] * 4 + [far] * 3 + [pl.BlockSpec(memory_space=pl.ANY)],
        out_specs=[near] * 3,
        scratch_shapes=[
            pltpu.VMEM((rank, rows, cols), jnp.float32),
            pltpu.VMEM((rows, cols), jnp.float32),
            pltpu.SemaphoreType.DMA((2,)),
        ],
        compiler_params=pltpu.CompilerParams(vmem_limit_bytes=26 * MIB),
        cost_estimate=pl.CostEstimate(flops=0, bytes_accessed=16 * waves * cells * 2, transcendentals=0),
        name="split",
    )(
        adjoint_now[0], adjoint_prev[0], source_now[0], source_prev[0],
        *map(in_hbm, (probe_left, probe_right, courant)),
        pair_edge,
    )
    inner = rows - 2 * edge
    rim = edge * cols

    def inner_kernel(begin, speed, out, saved, now, prev):
        now[...] = begin[...]
        a, b = now, prev
        for step in range(STEPS):
            saved[step, :2] = a[step : step + 2]
            saved[step, 2:] = a[rows - 2 - step : rows - step]
            advance_rows(step + 1, rows - 1 - step, a, b, speed, step == 0)
            a, b = b, a
        for r in range(edge, edge + inner):
            span = slice((r - edge) * cols, (r - edge + 1) * cols)
            inverse = 1.0 / speed[r : r + 1, :]
            out[0, :, span] = a[r] * inverse
            out[1, :, span] = b[r] * (-inverse)

    state = pltpu.VMEM((rows, rank, cols), jnp.float32)
    inner_own, saved = call(
        inner_kernel,
        [f32(2, rank, inner * cols), f32(STEPS, 4, rank, cols)],
        12,
        [state, state],
        name="probes_inner",
    )(start, courant)
    inner_other = lax.ppermute(inner_own, "shot", to_other)

    def far_speeds(pair, other):
        _, even = where_am_i()
        above = jnp.where(even, other[rank], pair[rank])
        below = jnp.where(even, pair[rank], other[rank])
        return above, below

    def rim_kernel(saved, speed, pair, other, out, up_now, up_prev, low_now, low_prev, up_speed, low_speed):
        _, even = where_am_i()
        up_speed[:edge, :], low_speed[edge + 1 :, :] = far_speeds(pair, other)
        up_speed[edge : 2 * edge, :] = speed[:edge, :]
        low_speed[1 : edge + 1, :] = speed[rows - edge :, :]
        from_pair = rows_first(pair[:rank] * pair[rank][None])
        from_other = rows_first(other[:rank] * other[rank][None])
        up_now[:edge] = jnp.where(even, from_other, from_pair)
        low_now[edge + 1 :] = jnp.where(even, from_pair, from_other)
        up_now[edge : edge + 2] = saved[0, :2]
        low_now[edge - 1 : edge + 1] = saved[0, 2:]
        a, b, c, d = up_now, up_prev, low_now, low_prev
        for step in range(1, STEPS + 1):
            advance_rows(step, edge + step, a, b, up_speed, step == 1)
            advance_rows(edge + 1 - step, 2 * edge + 1 - step, c, d, low_speed, step == 1)
            if step < STEPS:
                b[edge + step : edge + step + 2] = saved[step, :2]
                d[edge - 1 - step : edge + 1 - step] = saved[step, 2:]
            a, b, c, d = b, a, d, c
        for r in range(edge):
            upper = slice(r * cols, (r + 1) * cols)
            lower = slice(rim + r * cols, rim + (r + 1) * cols)
            inverse = 1.0 / speed[r : r + 1, :]
            out[0, :, upper] = a[edge + r] * inverse
            out[1, :, upper] = b[edge + r] * (-inverse)
            inverse = 1.0 / speed[rows - edge + r : rows - edge + r + 1, :]
            out[0, :, lower] = c[r + 1] * inverse
            out[1, :, lower] = d[r + 1] * (-inverse)

    short = pltpu.VMEM((2 * edge + 1, rank, cols), jnp.float32)
    short_speed = pltpu.VMEM((2 * edge + 1, cols), jnp.float32)
    rim_own = call(
        rim_kernel,
        f32(2, rank, 2 * rim),
        12,
        [short] * 4 + [short_speed] * 2,
        name="probes_rim",
    )(saved, courant, pair_halo, other_halo)
    rim_other = lax.ppermute(rim_own, "shot", to_other)

    def products(fields_ref, probes_ref, side, inside):
        total = jnp.zeros((2 * waves, 2 * rank), jnp.float32)
        places = [(rim, 0, inner * cols)] if inside else [(0, 0, rim), (cells - rim, rim, rim)]
        for level in range(2):
            for at, probe_at, count in places:
                pair = jnp.concatenate(parts_of(probes_ref[level, :, probe_at : probe_at + count], 2), 0)
                total = total + dot32(fields_ref[side, level, :, at : at + count], pair, NT)
        total = total[:waves] + total[waves:]
        return (total[:, :rank] + total[:, rank:]).T

    def product_kernel(fields_ref, inner_mine, inner_theirs, rim_mine, mine, theirs):
        side, _ = where_am_i()
        mine[...] = products(fields_ref, inner_mine, side, True) + products(
            fields_ref, rim_mine, side, False
        )
        theirs[...] = products(fields_ref, inner_theirs, 1 - side, True)

    half = rank // 2

    def product_last_kernel(fields_ref, rim_theirs, mine_ref, theirs_ref, out):
        side, _ = where_am_i()
        mine = mine_ref[...]
        theirs = theirs_ref[...] + products(fields_ref, rim_theirs, 1 - side, False)
        for shot in range(shots):
            weights = jnp.where(side == shot, mine, theirs)
            weights = jnp.concatenate([weights[:half], weights[half:]], 1)
            for strip in range(strips):
                out[shot * strips + strip] = weights

    flops = 2 * 2 * waves * 2 * rank * cells * 2
    mine, theirs = call(product_kernel, [f32(rank, waves)] * 2, 24, name="product")(
        fields, inner_own, inner_other, rim_own
    )
    pieces = call(
        product_last_kernel, f32(shots * strips, half, 2 * waves), 24, name="product_last"
    )(fields, rim_other, mine, theirs)
    stage, pieces = lax.optimization_barrier((stage, pieces))
    raw = lax.ppermute(stage, "shot", to_other)
    pieces = lax.all_to_all(pieces, ("shot", "strip"), 0, 0)

    def combine(pieces_ref, fields_ref, raw, blocks, out, swapped):
        side, _ = where_am_i()
        weights = []
        for shot in range(shots):
            packed = jnp.sum(pieces_ref[shot * strips : (shot + 1) * strips], 0)
            weights.append(jnp.concatenate([packed[:, :waves], packed[:, waves:]], 0))
        stacks = []
        for own, other in (weights, weights[::-1]):
            stack = jnp.concatenate(parts_of(jnp.where(side == 0, own, other), 2), 0)
            stacks.append(jnp.concatenate([stack, stack], 1))
        for level in range(2):
            for place, block in enumerate(blocks):
                here = slice(block * cols, (block + 8) * cols)
                there = slice(place * 8 * cols, (place + 1) * 8 * cols)
                for r in range(8):
                    high, low = parts_of(raw[level, block + r], 2)
                    span = slice((place * 8 + r) * cols, (place * 8 + r + 1) * cols)
                    swapped[level, :waves, span] = high
                    swapped[level, waves:, span] = low
                both = jnp.dot(
                    stacks[0], fields_ref[1 - side, level, :, here], preferred_element_type=jnp.float32
                ) + jnp.dot(stacks[1], swapped[level, :, there], preferred_element_type=jnp.float32)
                out[level, :, there] = both[:rank] + both[rank:]

    def rim_terms_kernel(pieces_ref, fields_ref, raw, out, swapped):
        blocks = [*range(0, edge, 8), *range(rows - edge, rows, 8)]
        combine(pieces_ref, fields_ref, raw, blocks, out, swapped)

    def inner_terms_kernel(pieces_ref, fields_ref, raw, _, out, swapped):
        combine(pieces_ref, fields_ref, raw, range(edge, rows - edge, 8), out, swapped)

    rim_terms = call(
        rim_terms_kernel,
        f32(2, rank, 2 * rim),
        24,
        [pltpu.VMEM((2, 2 * waves, 2 * rim), jnp.bfloat16)],
        name="terms_rim",
        flops=flops,
    )(pieces, fields, raw)

    def spill_kernel(
        own, speed, pair, other, pair_out, other_out, saved,
        up_now, up_prev, low_now, low_prev, up_speed, low_speed,
    ):
        _, even = where_am_i()
        above, below = far_speeds(pair, other)
        up_speed[1 : edge + 1, :] = above
        up_speed[edge + 1 :, :] = speed[:edge, :]
        low_speed[:edge, :] = speed[rows - edge :, :]
        low_speed[edge : 2 * edge, :] = below
        zeros = jnp.zeros((edge + 1, rank, cols), jnp.float32)
        for up, low, level in ((up_now, low_now, 0), (up_prev, low_prev, 1)):
            up[: edge + 1] = zeros
            low[edge:] = zeros
            for r in range(edge):
                span = slice(r * cols, (r + 1) * cols)
                up[edge + 1 + r] = own[level, :, span]
                span = slice(rim + r * cols, rim + (r + 1) * cols)
                low[r] = own[level, :, span]
        a, b, c, d = up_now, up_prev, low_now, low_prev
        for step in range(1, STEPS + 1):
            advance_rows(edge + 1 - step, 2 * edge + 1 - step, a, b, up_speed, False)
            advance_rows(step, edge + step, c, d, low_speed, False)
            if step < STEPS:
                saved[step - 1, :2] = b[2 * edge - 1 - step : 2 * edge + 1 - step]
                saved[step - 1, 2:] = d[step : step + 2]
            a, b, c, d = b, a, d, c
        pair_out[:, rim:] = jnp.zeros((rank, LANES), jnp.float32)
        for r in range(edge):
            span = slice(r * cols, (r + 1) * cols)
            upper, lower = a[1 + r], c[edge + r]
            pair_out[:, span] = jnp.where(even, lower, upper)
            other_out[:, span] = jnp.where(even, upper, lower)

    spill = f32(rank, rim)
    pair_spill, other_spill, spill_saved = call(
        spill_kernel,
        [f32(rank, rim + LANES), spill, f32(STEPS - 1, 4, rank, cols)],
        16,
        [short] * 4 + [short_speed] * 2,
        name="spill",
    )(rim_terms, courant, pair_halo, other_halo)
    other_add = lax.ppermute(other_spill, "strip", to_next)
    pair_add = lax.ppermute(pair_spill, "strip", to_pair)

    inner_terms = call(
        inner_terms_kernel,
        f32(2, rank, inner * cols),
        24,
        [pltpu.VMEM((2, 2 * waves, inner * cols), jnp.bfloat16)],
        name="terms_inner",
        flops=flops,
    )(pieces, fields, raw, pair_spill)
    def gram_of(piece):
        stack = jnp.concatenate(parts_of(piece, 3), 0)
        return dot32(stack, stack, NT)

    def sketch_kernel(rim_part, inner_part, speed, saved, out, gram_out, now, prev, speeds):
        speeds[1 : rows + 1, :] = speed[...]
        for r in range(edge - 2, rows - edge + 2):
            part, line = rim_part, r
            if edge <= r < rows - edge:
                part, line = inner_part, r - edge
            elif r >= edge:
                line = r - inner
            span = slice(line * cols, (line + 1) * cols)
            now[r + 1] = part[0, :, span]
            prev[r + 1] = part[1, :, span]
        a, b = now, prev
        for step in range(1, STEPS + 1):
            first, last = edge + 1 - step, rows - edge + 1 + step
            advance_rows(first, last, a, b, speeds, False)
            if step < STEPS:
                b[first - 2 : first] = saved[step - 1, :2]
                b[last : last + 2] = saved[step - 1, 2:]
            a, b = b, a
        for r in range(rows):
            out[:, r * cols : (r + 1) * cols] = a[r + 1]
        gram_out[...] = gram_of(out[:, rim : cells - rim])

    lines = pltpu.VMEM((rows + 2, rank, cols), jnp.float32)
    sketch_own, inner_gram = call(
        sketch_kernel,
        [f32(rank, cells), f32(3 * rank, 3 * rank)],
        16,
        [lines, lines, pltpu.VMEM((rows + 2, cols), jnp.float32)],
        name="sketch",
        moved=8 * MIB,
    )(rim_terms, inner_terms, courant, spill_saved)

    places = shots * strips

    def gram_kernel(own, pair, other, inner_total, out, pieces_out):
        _, even = where_am_i()
        top = own[:, :rim] + jnp.where(even, other[:, :rim], pair[:, :rim])
        bottom = own[:, cells - rim :] + jnp.where(even, pair[:, :rim], other[:, :rim])
        out[:, :rim] = top
        out[:, cells - rim :] = bottom
        total = inner_total[...] + gram_of(jnp.concatenate([top, bottom], 1))
        wide = total[:, :rank] + total[:, rank : 2 * rank] + total[:, 2 * rank :]
        gram = wide[:rank] + wide[rank : 2 * rank] + wide[2 * rank :]
        gram = jnp.concatenate(
            [gram[:half], gram[half:], jnp.zeros((half, LANES - 2 * rank), jnp.float32)], 1
        )
        for place in range(places):
            pieces_out[place] = gram

    sketch, gram_pieces = pl.pallas_call(
        gram_kernel,
        out_shape=[f32(rank, cells), f32(places, rank // 2, LANES)],
        in_specs=[near] * 4,
        out_specs=[near] * 2,
        input_output_aliases={0: 0},
        compiler_params=pltpu.CompilerParams(vmem_limit_bytes=12 * MIB),
        name="gram",
    )(sketch_own, pair_add, other_add, inner_gram)
    sketch_other = lax.ppermute(sketch, "shot", to_other)
    gram_pieces = lax.all_to_all(gram_pieces, ("shot", "strip"), 0, 0)

    def factor_kernel(grams, own, theirs, left_out, right_out, held, thick, sems):
        side, _ = where_am_i()
        for shot in range(2):
            for block in range(0, rows, 8):
                span = slice(block * cols, (block + 8) * cols)
                lines = jnp.where(side == shot, own[:, span], theirs[:, span])
                thick[shot, :, span] = jnp.concatenate(parts_of(lines, 2), 0)
        line = lax.broadcasted_iota(jnp.int32, (rank, rank), 0)
        column = lax.broadcasted_iota(jnp.int32, (rank, rank), 1)
        tall_line = lax.broadcasted_iota(jnp.int32, (rank, LANES), 0)
        sides = []
        for shot in range(2):
            halves = jnp.sum(grams[shot * strips : (shot + 1) * strips], 0)
            gram = jnp.concatenate([halves[:, :rank], halves[:, rank : 2 * rank]], 0)
            columns = [jnp.broadcast_to(gram[:, j : j + 1], (rank, LANES)) for j in range(rank)]
            sides.append((columns, [jnp.where(line == column, 1.0, 0.0)]))
        for j in range(rank):
            for columns, inverse in sides:
                factor = columns[j] * (1.0 / columns[j][j : j + 1])
                factor = jnp.where(tall_line > j, factor, 0.0)
                for k in range(j + 1, rank):
                    columns[k] = columns[k] - factor * columns[k][j : j + 1]
                inverse[0] = inverse[0] - factor[:, :rank] * inverse[0][j : j + 1]
        copies = []
        for (columns, inverse), shot, out in zip(sides, (0, 1), (left_out, right_out)):
            pivots = columns[0]
            for j in range(1, rank):
                pivots = jnp.where(tall_line == j, columns[j], pivots)
            inverse = inverse[0] * (lax.rsqrt(pivots[:, :rank]) * factor_scale)
            stack = jnp.concatenate(parts_of(inverse, 2), 0)
            stack = jnp.concatenate([stack] * 2, 1)
            for block in range(0, rows, 8):
                span = slice(block * cols, (block + 8) * cols)
                solved = jnp.dot(stack, thick[shot, :, span], preferred_element_type=jnp.float32)
                solved = solved[:rank] + solved[rank:]
                for t in range(0, cols, LANES):
                    tile = [solved[:, r * cols + t : r * cols + t + LANES][None] for r in range(8)]
                    held[shot, :, block : block + 8, t : t + LANES] = jnp.swapaxes(
                        jnp.concatenate(tile, 0), 0, 1
                    )
                lines_here = pl.ds(block, 8)
                copies.append(
                    pltpu.make_async_copy(
                        held.at[shot, :, lines_here], out.at[:, lines_here], sems.at[shot, block // 8]
                    )
                )
                copies[-1].start()
        for copy in copies:
            copy.wait()

    factor = f32(rank, rows, cols)
    left_factor, right_factor = pl.pallas_call(
        factor_kernel,
        out_shape=[factor, factor],
        in_specs=[near] * 3,
        out_specs=[far] * 2,
        scratch_shapes=[
            pltpu.VMEM((2, rank, rows, cols), jnp.float32),
            pltpu.VMEM((2, 2 * rank, cells), jnp.bfloat16),
            pltpu.SemaphoreType.DMA((2, rows // 8)),
        ],
        compiler_params=pltpu.CompilerParams(vmem_limit_bytes=12 * MIB),
        name="factors",
    )(gram_pieces, sketch, sketch_other)
    return left_factor, right_factor


def solution(mesh):
    return jax.shard_map(
        shards,
        mesh=mesh,
        in_specs=(
            P("shot", None, "strip", None),
            P("shot", None, "strip", None),
            P("shot", None, "strip", None),
            P("shot", None, "strip", None),
            P("strip", None),
            P(None, "strip", None),
            P(None, "strip", None),
        ),
        out_specs=(P(None, "strip", None), P(None, "strip", None)),
        check_vma=False,
    )
```
